512 devices in a mesh: dp: 64 (over x, y, core), tensor: 8 (over z).
Axes of the slice: x: 4, y: 8, z: 8, core: 2. Of those that a mesh axis runs over, the one named last changes fastest.
Arguments:
- acts: bfloat16 [65536, 4096], P(('dp', 'tensor')), may hold values from -6 to 6
- grad_out: bfloat16 [65536, 1024], P('dp', 'tensor'), may hold values from -0.1875 to 0.1875
- error: bfloat16 [64, 4096, 1024], P('dp', None, 'tensor'), may hold values from -6 to 6
- q_init: float32 [1024, 32], P('tensor'), may hold values from -0.5 to 0.5
Outputs:
- new_error: bfloat16 [64, 4096, 1024], P('dp', None, 'tensor')
- q_factor: float32 [1024, 32], P('tensor')
- p_basis: float32 [8, 4096, 32], P('tensor')
The draws below stay inside these ranges and needn't reach their ends.
All inputs are finite; a program needn't handle non-finite values.
Results may differ from the reference program's by a relative error of at most 0.00045.
Values may be sent and summed in bfloat16 or wider, within the bound.
A program may use at most 64 MiB of HBM per device.

```python
import jax
import jax.numpy as jnp
from jax import lax

D = 4096
HEAD = 128
HEADS_DEV = 1
RANK = 32
TOK_DEV = 1024
TOKENS = 65536
REPLICAS = 64
TP_SHARDS = 8
COLS = 1024


def shard_levels(key, extent, shards, least, high):
    def one(dim, shards_of):
        heights = jax.random.uniform(jax.random.fold_in(jax.random.fold_in(key, 6), dim), (shards_of,), jnp.float32, least / len(shards), high / len(shards))
        return jnp.repeat(jnp.exp(heights), extent[dim] // shards_of).reshape((-1,) + (1,) * (len(extent) - dim - 1))

    factor_of = one(*shards[0])
    for cut in shards[1:]:
        factor_of = factor_of * one(*cut)
    return factor_of


def bell_draw(rng, shape, scale, limit, split=(), kind=jnp.bfloat16):
    gain = shard_levels(rng, shape, split, -0.22, 0.18) if split else 1.0
    drawn = jax.random.normal(rng, shape, jnp.float32) * scale * gain
    return jnp.minimum(jnp.maximum(drawn, -limit), limit).astype(kind)


def setup_inputs(seed: int = 0) -> dict:
    key_of = jax.random.split(jax.random.key(seed), 5)
    return {
        "acts": bell_draw(key_of[0], (TOKENS, D), 1.0, 6.0, ((0, 512),)),
        "grad_out": bell_draw(key_of[1], (TOKENS, COLS), TOK_DEV ** -0.5, 0.1875, ((0, 64), (1, 8))),
        "error": bell_draw(key_of[2], (REPLICAS, D, COLS), 1.0, 6.0, ((0, 64), (2, 8))),
        "q_init": bell_draw(key_of[3], (COLS, RANK), (HEAD * HEADS_DEV) ** -0.5, 0.5, ((0, 8),), jnp.float32),
    }


def merged_of(index, acts, grad_out, error):
    start = (index * TOK_DEV).astype(jnp.int32)
    rows_x = lax.dynamic_slice_in_dim(acts, start, TOK_DEV, 0)
    rows_y = lax.dynamic_slice_in_dim(grad_out, start, TOK_DEV, 0)
    grad = jnp.dot(rows_x.T.astype(jnp.float32), rows_y.astype(jnp.float32), preferred_element_type=jnp.float32)
    merged = grad + error[index].astype(jnp.float32)
    return merged.reshape(D, TP_SHARDS, HEAD * HEADS_DEV)

def reference(acts, grad_out, error, q_init):
    width = HEAD * HEADS_DEV
    starts = jnp.arange(REPLICAS, dtype=jnp.int32)
    q_start = q_init.reshape(TP_SHARDS, width, RANK)

    def add_p(carry, index):
        merged = merged_of(index, acts, grad_out, error)
        term = jnp.einsum('dtc,tck->tdk', merged, q_start, precision=lax.Precision.HIGHEST)
        return (carry + term, None)
    p_sum, _ = lax.scan(add_p, jnp.zeros((TP_SHARDS, D, RANK), jnp.float32), starts)
    gram = jnp.einsum('tdk,tdj->tkj', p_sum, p_sum, precision=lax.Precision.HIGHEST)
    lower = jnp.linalg.cholesky(gram)

    def solve_one(factor, chol):
        return lax.linalg.triangular_solve(chol, factor, left_side=False, lower=True, transpose_a=True)
    p_basis = jax.vmap(solve_one)(p_sum, lower)

    def add_q(carry, index):
        merged = merged_of(index, acts, grad_out, error)
        term = jnp.einsum('dtc,tdk->tck', merged, p_basis, precision=lax.Precision.HIGHEST)
        return (carry + term, None)
    q_total, _ = lax.scan(add_q, jnp.zeros((TP_SHARDS, width, RANK), jnp.float32), starts)
    update = jnp.einsum('tdk,tck->dtc', p_basis, q_total, precision=lax.Precision.HIGHEST) / REPLICAS

    def renew(index):
        merged = merged_of(index, acts, grad_out, error)
        return (merged - update).astype(jnp.bfloat16).reshape(D, COLS)
    new_error = lax.map(renew, starts)
    return (new_error, q_total.reshape(COLS, RANK), p_basis)
```

```python
import jax
import jax.numpy as jnp
from jax import lax
from jax.experimental import pallas as pl
from jax.experimental.pallas import tpu as pltpu
from jax.sharding import PartitionSpec as P

NX, NY, NC, NZ = 4, 8, 2, 8
D, HEAD, RANK, TOK = 4096, 128, 32, 1024
BLOCK = TOK // NZ
CHUNKS = 8
WIDE = D // CHUNKS
HALF = WIDE // NC
ROWS_Y = HALF // NY
ROWS_X = ROWS_Y // NX
TILES = CHUNKS * RANK // HEAD
PER = CHUNKS // TILES
HIGHEST = lax.Precision.HIGHEST
MESH = pl.DeviceIdType.MESH


def dot(a, b, dims=((1,), (0,))):
    return lax.dot_general(a, b, (dims, ((), ())), precision=HIGHEST, preferred_element_type=jnp.float32)


def eliminate(gram, right):
    n = RANK
    row = lax.broadcasted_iota(jnp.int32, (n, n), 0)
    col = lax.broadcasted_iota(jnp.int32, (n, n), 1)
    left = jnp.concatenate([gram, jnp.where(row == col, 1.0, 0.0).astype(jnp.float32)], axis=1)
    rows = lax.broadcasted_iota(jnp.int32, (n, 1), 0)
    for j in range(n):
        inv = 1.0 / jnp.sqrt(left[j : j + 1, j : j + 1])
        pivot_l = left[j : j + 1, :] * inv
        pivot_r = right[j : j + 1, :] * inv
        factor = left[:, j : j + 1] * inv
        below = rows > j
        same = rows == j
        left = jnp.where(below, left - factor * pivot_l, jnp.where(same, pivot_l, left))
        right = jnp.where(below, right - factor * pivot_r, jnp.where(same, pivot_r, right))
    return left[:, n:], right


def kernel(
    acts, grad_out, error, q_init,
    new_error, q_out, p_out,
    abuf, gbuf, ebuf, merged, nbuf, core_in, core_sum, y_in, y_sum, x_in, own, pg, qcore, qy, qx,
    load_sem, g_sem, e_sem, out_sem, z_send, z_recv, c_send, c_recv, y_send, y_recv, x_send, x_recv,
    p_send, p_recv, q_send, q_recv,
):
    dp = lax.axis_index("dp")
    z = lax.axis_index("tensor")
    core = lax.rem(dp, NC)
    y = lax.rem(dp // NC, NY)
    x = dp // (NC * NY)

    def at(x_, y_, core_):
        return ((x_ * NY + y_) * NC + core_, z)

    up = (dp, lax.rem(z + 1, NZ))
    down = (dp, lax.rem(z + NZ - 1, NZ))
    sibling = at(x, y, 1 - core)
    ys = [(lax.rem(y + k, NY), at(x, lax.rem(y + k, NY), core)) for k in range(1, NY)]
    xs = [(lax.rem(x + k, NX), at(lax.rem(x + k, NX), y, core)) for k in range(1, NX)]

    def load(c):
        columns = pl.ds(pl.multiple_of(c * WIDE, WIDE), WIDE)
        return pltpu.make_async_copy(acts.at[:, columns], abuf.at[c, z], load_sem.at[c])

    @pl.loop(0, CHUNKS)
    def _(c):
        load(c).start()

    load_g = pltpu.make_async_copy(grad_out, gbuf, g_sem)
    load_e = pltpu.make_async_copy(error, ebuf, e_sem)
    load_g.start()
    load_e.start()

    barrier = pltpu.get_barrier_semaphore()
    partners = [up, down, sibling] + [d for _, d in ys] + [d for _, d in xs]
    for device in partners:
        pl.semaphore_signal(barrier, inc=1, device_id=device, device_id_type=MESH)
    pl.semaphore_wait(barrier, len(partners))

    def piece(c, slot, hop, way):
        if hop < 4:
            return abuf.at[c, slot]
        return abuf.at[c, slot, pl.ds(way * (BLOCK // 2), BLOCK // 2)]

    def z_copy(c, hop, way, sending):
        step = hop - 1 if sending else hop
        slot = lax.rem(z + (NZ - step if way == 0 else step), NZ)
        ref = piece(c, slot, hop, way)
        return pltpu.make_async_remote_copy(
            src_ref=ref, dst_ref=ref,
            send_sem=z_send.at[way, hop - 1, c], recv_sem=z_recv.at[way, hop - 1, c],
            device_id=up if way == 0 else down, device_id_type=MESH,
        )

    def to(ref_from, ref_to, send_sem, recv_sem, device):
        return pltpu.make_async_remote_copy(
            src_ref=ref_from, dst_ref=ref_to, send_sem=send_sem, recv_sem=recv_sem,
            device_id=device, device_id_type=MESH,
        )

    def wait_bytes(ref, sem):
        pltpu.make_async_copy(ref, ref, sem).wait()

    def rows_of(c, start, size):
        return pl.ds(pl.multiple_of(c * WIDE + start, 8), size)

    def core_copy(c):
        return to(
            merged.at[rows_of(c, (1 - core) * HALF, HALF)], core_in.at[c],
            c_send.at[c], c_recv.at[c], sibling,
        )

    def on(c, act):
        pl.when(jnp.logical_and(c >= 0, c < CHUNKS))(lambda: act(c))

    def own_send(c):
        load(c).wait()
        for way in range(2):
            z_copy(c, 1, way, True).start()

    def forward(hop):
        def act(c):
            for way in range(2):
                z_copy(c, hop, way, False).wait_recv()
                z_copy(c, hop + 1, way, True).start()
        return act

    def multiply(c):
        for way in range(2):
            z_copy(c, 4, way, False).wait_recv()
        grad = lax.dot_general(
            abuf[c].reshape(TOK, WIDE), gbuf[...], (((0,), (0,)), ((), ())),
            preferred_element_type=jnp.float32,
        )
        rows = rows_of(c, 0, WIDE)
        merged[rows, :] = grad + ebuf[rows, :].astype(jnp.float32)
        core_copy(c).start()

    def sum_core(c):
        core_copy(c).wait_recv()
        core_sum[c] = merged[rows_of(c, core * HALF, HALF), :] + core_in[c]
        for k, (other, device) in enumerate(ys):
            part = pl.ds(pl.multiple_of(other * ROWS_Y, ROWS_Y), ROWS_Y)
            to(core_sum.at[c, part], y_in.at[c, k], y_send.at[c], y_recv.at[c], device).start()

    def sum_y(c):
        wait_bytes(y_in.at[c], y_recv.at[c])
        total = core_sum[c, pl.ds(pl.multiple_of(y * ROWS_Y, ROWS_Y), ROWS_Y), :]
        for k in range(NY - 1):
            total = total + y_in[c, k]
        y_sum[c] = total
        for k, (other, device) in enumerate(xs):
            part = pl.ds(pl.multiple_of(other * ROWS_X, ROWS_X), ROWS_X)
            to(y_sum.at[c, part], x_in.at[c, k], x_send.at[c], x_recv.at[c], device).start()

    def sum_x(c):
        wait_bytes(x_in.at[c], x_recv.at[c])
        total = y_sum[c, pl.ds(pl.multiple_of(x * ROWS_X, ROWS_X), ROWS_X), :]
        for k in range(NX - 1):
            total = total + x_in[c, k]
        own[pl.ds(pl.multiple_of(c * ROWS_X, ROWS_X), ROWS_X), :] = total

    @pl.loop(0, CHUNKS + 6)
    def _(k):
        on(k, own_send)
        pl.when(k == 3)(lambda: (load_g.wait(), load_e.wait())[0])
        on(k - 1, forward(1))
        on(k - 5, sum_core)
        on(k - 2, forward(2))
        on(k - 6, sum_x)
        on(k - 3, forward(3))
        on(k - 5, sum_y)
        on(k - 4, multiply)

    m_own = own[...]
    p_own = dot(m_own, q_init[...])
    q_part = dot(p_own, m_own, ((0,), (0,)))
    qcore[0] = q_part
    q_c = to(qcore.at[0], qcore.at[1], q_send.at[0], q_recv.at[0], sibling)
    q_c.start()

    for t in range(TILES):
        pg[t, core, y, x] = jnp.concatenate(
            [p_own[(t * PER + j) * ROWS_X : (t * PER + j + 1) * ROWS_X, :] for j in range(PER)], axis=1
        )
        for _, device in xs:
            to(pg.at[t, core, y, x], pg.at[t, core, y, x], p_send.at[0, t], p_recv.at[0, t], device).start()

    q_c.wait_recv()
    qy[y] = qcore[0] + qcore[1]
    for _, device in ys:
        to(qy.at[y], qy.at[y], q_send.at[1], q_recv.at[1], device).start()

    for t in range(TILES):
        wait_bytes(pg.at[t, core, y, pl.ds(0, NX - 1)], p_recv.at[0, t])
        for _, device in ys:
            to(pg.at[t, core, y], pg.at[t, core, y], p_send.at[1, t], p_recv.at[1, t], device).start()

    wait_bytes(qy.at[pl.ds(0, NY - 1)], q_recv.at[1])
    total = qy[0]
    for k in range(1, NY):
        total = total + qy[k]
    qx[x] = total
    for _, device in xs:
        to(qx.at[x], qx.at[x], q_send.at[2], q_recv.at[2], device).start()

    for t in range(TILES):
        wait_bytes(pg.at[t, core, pl.ds(0, NY - 1)], p_recv.at[1, t])
        to(pg.at[t, core], pg.at[t, core], p_send.at[2, t], p_recv.at[2, t], sibling).start()

    wait_bytes(qx.at[pl.ds(0, NX - 1)], q_recv.at[2])
    q_t = qx[0]
    for k in range(1, NX):
        q_t = q_t + qx[k]

    gram = dot(q_t, q_init[...])
    inverse, q_fac = eliminate(gram, q_t)
    q_out[...] = q_fac
    back = dot(inverse, q_fac, ((0,), (0,))) * (1.0 / (NX * NY * NC))

    def spread(small):
        width = small.shape[1]
        tall = jnp.concatenate([small] * PER, axis=0)
        wide = jnp.concatenate([tall] * PER, axis=1)
        group_r = lax.broadcasted_iota(jnp.int32, wide.shape, 0) // RANK
        group_c = lax.broadcasted_iota(jnp.int32, wide.shape, 1) // width
        return jnp.where(group_r == group_c, wide, 0.0)

    to_basis = spread(inverse.T)
    to_update = spread(back)

    for t in range(TILES):
        to(pg.at[t, core], pg.at[t, 1 - core], p_send.at[2, t], p_recv.at[2, t], sibling).wait_recv()
        p_sum = pg[t].reshape(WIDE, HEAD)
        update = dot(p_sum, to_update)
        for j in range(PER):
            rows = pl.ds((t * PER + j) * WIDE, WIDE)
            nbuf[rows, :] = (merged[rows, :] - update[:, j * HEAD : (j + 1) * HEAD]).astype(jnp.bfloat16)
            pltpu.make_async_copy(nbuf.at[rows], new_error.at[rows], out_sem.at[t * PER + j]).start()
        p_out[t] = dot(p_sum, to_basis)

    @pl.loop(0, CHUNKS)
    def _(c):
        for way in range(2):
            for hop in range(1, 5):
                z_copy(c, hop, way, True).wait_send()
        core_copy(c).wait_send()
        wait_bytes(y_in.at[c], y_send.at[c])
        wait_bytes(x_in.at[c], x_send.at[c])
        rows = rows_of(c, 0, WIDE)
        pltpu.make_async_copy(nbuf.at[rows], new_error.at[rows], out_sem.at[c]).wait()
    for t in range(TILES):
        wait_bytes(pg.at[t, core, y, pl.ds(0, NX - 1)], p_send.at[0, t])
        wait_bytes(pg.at[t, core, pl.ds(0, NY - 1)], p_send.at[1, t])
        wait_bytes(pg.at[t, core], p_send.at[2, t])
    q_c.wait_send()
    wait_bytes(qy.at[pl.ds(0, NY - 1)], q_send.at[1])
    wait_bytes(qx.at[pl.ds(0, NX - 1)], q_send.at[2])


def per_device(acts, grad_out, error, q_init):
    f32, bf16 = jnp.float32, jnp.bfloat16
    dma = pltpu.SemaphoreType.DMA
    anywhere = pl.BlockSpec(memory_space=pl.ANY)
    vmem = pl.BlockSpec(memory_space=pltpu.VMEM)
    new_error, q_t, p_packed = pl.pallas_call(
        kernel,
        out_shape=(
            jax.ShapeDtypeStruct((D, HEAD), bf16),
            jax.ShapeDtypeStruct((RANK, HEAD), f32),
            jax.ShapeDtypeStruct((TILES, WIDE, HEAD), f32),
        ),
        in_specs=[anywhere, anywhere, anywhere, vmem],
        out_specs=(anywhere, vmem, vmem),
        scratch_shapes=[
            pltpu.VMEM((CHUNKS, NZ, BLOCK, WIDE), bf16),
            pltpu.VMEM((TOK, HEAD), bf16),
            pltpu.VMEM((D, HEAD), bf16),
            pltpu.VMEM((D, HEAD), f32),
            pltpu.VMEM((D, HEAD), bf16),
            pltpu.VMEM((CHUNKS, HALF, HEAD), f32),
            pltpu.VMEM((CHUNKS, HALF, HEAD), f32),
            pltpu.VMEM((CHUNKS, NY - 1, ROWS_Y, HEAD), f32),
            pltpu.VMEM((CHUNKS, ROWS_Y, HEAD), f32),
            pltpu.VMEM((CHUNKS, NX - 1, ROWS_X, HEAD), f32),
            pltpu.VMEM((CHUNKS * ROWS_X, HEAD), f32),
            pltpu.VMEM((TILES, NC, NY, NX, ROWS_X, HEAD), f32),
            pltpu.VMEM((2, RANK, HEAD), f32),
            pltpu.VMEM((NY, RANK, HEAD), f32),
            pltpu.VMEM((NX, RANK, HEAD), f32),
            dma((CHUNKS,)), dma, dma, dma((CHUNKS,)),
            dma((2, 4, CHUNKS)), dma((2, 4, CHUNKS)),
            dma((CHUNKS,)), dma((CHUNKS,)),
            dma((CHUNKS,)), dma((CHUNKS,)),
            dma((CHUNKS,)), dma((CHUNKS,)),
            dma((3, TILES)), dma((3, TILES)),
            dma((3,)), dma((3,)),
        ],
        compiler_params=pltpu.CompilerParams(
            collective_id=0, has_side_effects=True, vmem_limit_bytes=48 * 2**20
        ),
    )(acts, grad_out, error[0], q_init)
    p_basis = p_packed.reshape(TILES, WIDE, PER, RANK).transpose(0, 2, 1, 3).reshape(1, D, RANK)
    return new_error[None], q_t.T, p_basis


def solution(mesh):
    return jax.shard_map(
        per_device,
        mesh=mesh,
        in_specs=(
            P(("dp", "tensor"), None),
            P("dp", "tensor"),
            P("dp", None, "tensor"),
            P("tensor", None),
        ),
        out_specs=(P("dp", None, "tensor"), P("tensor", None), P("tensor", None, None)),
        check_vma=False,
    )
```

```python
import jax
import jax.numpy as jnp
from jax import lax
from jax.experimental import pallas as pl
from jax.experimental.pallas import tpu as pltpu
from jax.sharding import PartitionSpec as P

NX, NY, NC, NZ = 4, 8, 2, 8
D, HEAD, RANK, TOK = 4096, 128, 32, 1024
BLOCK = TOK // NZ
CHUNKS = 8
WIDE = D // CHUNKS
LANES = WIDE // NX
PART = RANK // NC
F32, BF16 = jnp.float32, jnp.bfloat16
HIGHEST = lax.Precision.HIGHEST
MESH = pl.DeviceIdType.MESH
NT = ((1,), (1,))
NN = ((1,), (0,))
TN = ((0,), (0,))


def exact(a, b, dims=NN):
    return lax.dot_general(a, b, (dims, ((), ())), precision=HIGHEST, preferred_element_type=F32)


def single(a, b, dims=NN):
    return lax.dot_general(a, b, (dims, ((), ())), preferred_element_type=F32)


def split(value, parts):
    out = []
    for _ in range(parts):
        out.append(value.astype(BF16))
        value = value - out[-1].astype(F32)
    return out


def inverse_factor(gram):
    n = RANK
    row = lax.broadcasted_iota(jnp.int32, (n, n), 0)
    col = lax.broadcasted_iota(jnp.int32, (n, n), 1)
    both = jnp.concatenate([gram, jnp.where(row == col, 1.0, 0.0).astype(F32)], axis=1)
    rows = lax.broadcasted_iota(jnp.int32, (n, 1), 0)
    for j in range(n):
        inv = 1.0 / jnp.sqrt(both[j : j + 1, j : j + 1])
        pivot = both[j : j + 1, :] * inv
        factor = both[:, j : j + 1] * inv
        both = jnp.where(rows > j, both - factor * pivot, jnp.where(rows == j, pivot, both))
    return both[:, n:]


def kernel(
    acts, grad_out, error, q_init,
    new_error, q_out, p_out,
    abuf, gbuf, ebuf, qbuf, merged,
    w_out, w_in, w_split, partial, core_in, core_sum, x_in, x_sum, y_in, y_sum, z_in,
    pg, pt, pb, pb_rows, q_acc, q_core, qx_a, qy_a, qy_b, qx_b,
    load_sem, g_sem, e_sem, i_sem, z_send, z_recv, w_send, w_recv,
    c_send, c_recv, x_send, x_recv, y_send, y_recv, s_send, s_recv, p_send, p_recv, q_send, q_recv,
):
    dp = lax.axis_index("dp")
    z = lax.axis_index("tensor")
    core = lax.rem(dp, NC)
    y = lax.rem(dp // NC, NY)
    x = dp // (NC * NY)

    def at(x_, y_, core_):
        return ((x_ * NY + y_) * NC + core_, z)

    sibling = at(x, y, 1 - core)
    ys = [at(x, lax.rem(y + k, NY), core) for k in range(1, NY)]
    xs = [at(lax.rem(x + k, NX), y, core) for k in range(1, NX)]
    zs = [(dp, lax.rem(z + k, NZ)) for k in range(1, NZ)]
    up, down = zs[0], zs[-1]

    def to(ref_from, ref_to, send_sem, recv_sem, device):
        return pltpu.make_async_remote_copy(
            src_ref=ref_from, dst_ref=ref_to, send_sem=send_sem, recv_sem=recv_sem,
            device_id=device, device_id_type=MESH,
        )

    def wait_bytes(ref, sem):
        pltpu.make_async_copy(ref, ref, sem).wait()

    def load(c):
        columns = pl.ds(pl.multiple_of(c * WIDE, WIDE), WIDE)
        return pltpu.make_async_copy(acts.at[:, columns], abuf.at[c, z], load_sem.at[c])

    load_q = pltpu.make_async_copy(q_init, qbuf, i_sem)
    load_g = pltpu.make_async_copy(grad_out, gbuf, g_sem)
    load_e = pltpu.make_async_copy(error, ebuf, e_sem)
    load_q.start()
    load_g.start()

    @pl.loop(0, CHUNKS)
    def _(c):
        load(c).start()

    load_e.start()

    barrier = pltpu.get_barrier_semaphore()
    partners = [sibling] + ys + xs + zs
    for device in partners:
        pl.semaphore_signal(barrier, inc=1, device_id=device, device_id_type=MESH)

    load_q.wait()
    load_g.wait()
    q_parts = jnp.concatenate(split(qbuf[...], 3), axis=0)
    w_all = single(q_parts, gbuf[...], NT)
    w_all = w_all[:RANK] + w_all[RANK : 2 * RANK] + w_all[2 * RANK :]
    for s in range(NZ):
        for h in range(NC):
            w_out[s, h] = w_all[h * PART : (h + 1) * PART, s * BLOCK : (s + 1) * BLOCK]

    @pl.loop(0, CHUNKS)
    def _(c):
        load(c).wait()

    pl.semaphore_wait(barrier, len(partners))

    def w_copy(k):
        return to(w_out.at[lax.rem(z + k, NZ)], w_in.at[:, z], w_send.at[k - 1], w_recv, zs[k - 1])

    for k in range(1, NZ):
        w_copy(k).start()
    w_in[:, z] = w_out[z]

    def z_copy(c, hop, way, sending):
        step = hop - 1 if sending else hop
        slot = lax.rem(z + (NZ - step if way == 0 else step), NZ)
        ref = abuf.at[c, slot]
        if hop == 4:
            ref = abuf.at[c, slot, pl.ds(way * (BLOCK // 2), BLOCK // 2)]
        return to(ref, ref, z_send.at[way, hop - 1, c], z_recv.at[way, hop - 1, c], up if way == 0 else down)

    def on(c, act):
        pl.when(jnp.logical_and(c >= 0, c < CHUNKS))(lambda: act(c))

    def own_send(c):
        for way in range(2):
            z_copy(c, 1, way, True).start()

    def forward(hop):
        def act(c):
            for way in range(2):
                z_copy(c, hop, way, False).wait_recv()
                z_copy(c, hop + 1, way, True).start()
        return act

    def rows_of(c):
        return pl.ds(pl.multiple_of(c * WIDE, WIDE), WIDE)

    def multiply(c):
        for way in range(2):
            z_copy(c, 4, way, False).wait_recv()
        grad = single(abuf[c].reshape(TOK, WIDE), gbuf[...], TN)
        merged[rows_of(c), :] = grad + ebuf[rows_of(c), :].astype(F32)

    def w_ready():
        wait_bytes(w_in.at[:, pl.ds(0, NZ - 1)], w_recv)
        load_e.wait()
        w = w_in[...].reshape(NZ * RANK, BLOCK)
        for part, value in enumerate(split(w, 3)):
            w_split[part] = value

    def core_copy(i):
        return to(partial.at[i, 1 - core], core_in.at[i], c_send.at[i], c_recv.at[i], sibling)

    def p_partial(i):
        c = lax.rem(y + 1 + i, CHUNKS)
        a = abuf[c, z]
        total = single(w_split[0], a) + (single(w_split[1], a) + single(w_split[2], a))
        partial[i] = total.reshape(NC, NZ * PART, WIDE)
        e_all = single(jnp.concatenate(split(qbuf[...], 3), axis=0), ebuf[rows_of(c), :], NT)
        e_all = e_all[:RANK] + (e_all[RANK : 2 * RANK] + e_all[2 * RANK :])
        mine = pl.ds(pl.multiple_of(z * PART, PART), PART)
        for h in range(NC):
            partial[i, h, mine, :] = partial[i, h, mine, :] + e_all[h * PART : (h + 1) * PART]
        core_copy(i).start()

    def p_core(i):
        core_copy(i).wait_recv()
        total = partial[i, core] + core_in[i]
        for j in range(NX):
            core_sum[i, j] = total[:, j * LANES : (j + 1) * LANES]
        for k in range(1, NX):
            to(core_sum.at[i, lax.rem(x + k, NX)], x_in.at[i, k - 1], x_send.at[i], x_recv.at[i], xs[k - 1]).start()

    def y_copy(i):
        device = at(x, lax.rem(y + 1 + i, NY), core)
        return to(x_sum.at[i], y_in.at[i], y_send.at[i], y_recv, device)

    def p_x(i):
        wait_bytes(x_in.at[i], x_recv.at[i])
        total = core_sum[i, x]
        for k in range(NX - 1):
            total = total + x_in[i, k]
        x_sum[i] = total
        pl.when(i < CHUNKS - 1)(lambda: y_copy(i).start())

    def s_copy(k):
        return to(y_sum.at[lax.rem(z + k, NZ)], z_in.at[k - 1], s_send.at[k - 1], s_recv, zs[k - 1])

    def p_y():
        wait_bytes(y_in, y_recv)
        total = x_sum[CHUNKS - 1]
        for k in range(NY - 1):
            total = total + y_in[k]
        y_sum[...] = total.reshape(NZ, PART, LANES)
        for k in range(1, NZ):
            s_copy(k).start()

    def p_z():
        wait_bytes(z_in, s_recv)
        total = y_sum[z]
        for k in range(NZ - 1):
            total = total + z_in[k]
        mine = pg.at[core, y, x]
        mine[...] = total
        for device in xs:
            to(mine, mine, p_send.at[0], p_recv.at[0], device).start()

    def gather_y():
        wait_bytes(pg.at[core, y, pl.ds(0, NX - 1)], p_recv.at[0])
        for device in ys:
            to(pg.at[core, y], pg.at[core, y], p_send.at[1], p_recv.at[1], device).start()

    def gather_core():
        wait_bytes(pg.at[core, pl.ds(0, NY - 1)], p_recv.at[1])
        to(pg.at[core], pg.at[core], p_send.at[2], p_recv.at[2], sibling).start()

    def gather_done():
        wait_bytes(pg.at[core], p_recv.at[2])

        @pl.loop(0, CHUNKS)
        def _(c):
            for h in range(NC):
                for j in range(NX):
                    pt[c, h * PART : (h + 1) * PART, j * LANES : (j + 1) * LANES] = pg[h, c, j]

    def basis():
        tall = pt[...].reshape(CHUNKS * RANK, WIDE)
        square = exact(tall, tall, NT)
        gram = square[:RANK, :RANK]
        for c in range(1, CHUNKS):
            gram = gram + square[c * RANK : (c + 1) * RANK, c * RANK : (c + 1) * RANK]
        inverse = inverse_factor(gram)
        wide = jnp.concatenate([jnp.concatenate([inverse] * CHUNKS, axis=0)] * CHUNKS, axis=1)
        group_r = lax.broadcasted_iota(jnp.int32, wide.shape, 0) // RANK
        group_c = lax.broadcasted_iota(jnp.int32, wide.shape, 1) // RANK
        blocks = jnp.where(group_r == group_c, wide, 0.0)
        pb[...] = exact(blocks, tall).reshape(CHUNKS, RANK, WIDE)

    def basis_rows():
        @pl.loop(0, CHUNKS)
        def _(c):
            value = pb[c]
            p_out[:, rows_of(c)] = value
            high, low = [part.astype(F32) for part in split(value, 2)]
            stacked = jnp.concatenate([high, low, high, low], axis=0)
            pb_rows[rows_of(c), :] = stacked.T.astype(BF16)

        q_acc[...] = jnp.zeros_like(q_acc)

    def q_part(c):
        high, low = split(pb[c], 2)
        m_high, m_low = split(merged[rows_of(c), :], 2)
        first = single(jnp.concatenate([high, low], axis=0), m_high)
        q_acc[...] += first[:RANK] + (first[RANK:] + single(high, m_low))

    READY = 9

    def q_early(k):
        @pl.loop(0, READY - 4)
        def _(c):
            q_part(c)

    own_send(0)

    @pl.loop(0, CHUNKS + 4)
    def _(k):
        on(k + 1, own_send)
        pl.when(k == 1)(w_ready)
        on(2 * k - 2, p_partial)
        on(2 * k - 3, p_x)
        pl.when(k == 8)(gather_core)
        on(k - 1, forward(1))
        on(2 * k - 2, p_core)
        on(2 * k - 1, p_partial)
        pl.when(k == 7)(gather_y)
        pl.when(k == 8)(gather_done)
        on(k - 2, forward(2))
        on(2 * k - 1, p_core)
        pl.when(k == 8)(basis)
        on(k - 3, forward(3))
        on(2 * k - 2, p_x)
        pl.when(k == 5)(p_y)
        pl.when(k == 6)(p_z)
        pl.when(k == READY)(basis_rows)
        pl.when(k == READY)(lambda: q_early(k))
        on(k - 4, multiply)
        pl.when(k >= READY)(lambda: q_part(k - 4))

    q_core[0] = q_acc[...]
    q_c = to(q_core.at[0], q_core.at[1], q_send.at[0], q_recv.at[0], sibling)
    q_c.start()
    q_c.wait_recv()
    both = q_core[0] + q_core[1]

    def share(buf, place, value, sem, devices):
        buf[place] = value
        for device in devices:
            to(buf.at[place], buf.at[place], q_send.at[sem], q_recv.at[sem], device).start()

    def total_of(buf, sem):
        n = buf.shape[0]
        wait_bytes(buf.at[pl.ds(0, n - 1)], q_recv.at[sem])
        total = buf[0]
        for k in range(1, n):
            total = total + buf[k]
        return total

    share(qy_b, y, both[PART:], 2, ys)
    share(qx_a, x, both[:PART], 1, xs)
    share(qy_a, y, total_of(qx_a, 1), 3, ys)
    share(qx_b, x, total_of(qy_b, 2), 4, xs)
    q_t = jnp.concatenate([total_of(qy_a, 3), total_of(qx_b, 4)], axis=0)
    q_out[...] = q_t

    high, low = split(q_t * (1.0 / (NX * NY * NC)), 2)
    back = jnp.concatenate([high, high, low, low], axis=0)

    @pl.loop(0, CHUNKS)
    def _(c):
        update = single(pb_rows[rows_of(c), :], back)
        new_error[rows_of(c), :] = (merged[rows_of(c), :] - update).astype(BF16)

    @pl.loop(0, CHUNKS)
    def _(c):
        for way in range(2):
            for hop in range(1, 5):
                z_copy(c, hop, way, True).wait_send()
        core_copy(c).wait_send()
        wait_bytes(x_in.at[c], x_send.at[c])
        pl.when(c < CHUNKS - 1)(lambda: y_copy(c).wait_send())

    for k in range(1, NZ):
        w_copy(k).wait_send()
        s_copy(k).wait_send()
    wait_bytes(pg.at[core, y, pl.ds(0, NX - 1)], p_send.at[0])
    wait_bytes(pg.at[core, pl.ds(0, NY - 1)], p_send.at[1])
    wait_bytes(pg.at[core], p_send.at[2])
    q_c.wait_send()
    wait_bytes(qx_a.at[pl.ds(0, NX - 1)], q_send.at[1])
    wait_bytes(qy_b.at[pl.ds(0, NY - 1)], q_send.at[2])
    wait_bytes(qy_a.at[pl.ds(0, NY - 1)], q_send.at[3])
    wait_bytes(qx_b.at[pl.ds(0, NX - 1)], q_send.at[4])


def per_device(acts, grad_out, error, q_init):
    dma = pltpu.SemaphoreType.DMA
    hbm = pl.BlockSpec(memory_space=pltpu.HBM)
    vmem = pl.BlockSpec(memory_space=pltpu.VMEM)
    new_error, q_t, p_t = pl.pallas_call(
        kernel,
        out_shape=(
            jax.ShapeDtypeStruct((D, HEAD), BF16),
            jax.ShapeDtypeStruct((RANK, HEAD), F32),
            jax.ShapeDtypeStruct((RANK, D), F32),
        ),
        in_specs=[hbm, hbm, hbm, hbm],
        out_specs=(vmem, vmem, vmem),
        scratch_shapes=[
            pltpu.VMEM((CHUNKS, NZ, BLOCK, WIDE), BF16),
            pltpu.VMEM((TOK, HEAD), BF16),
            pltpu.VMEM((D, HEAD), BF16),
            pltpu.VMEM((RANK, HEAD), F32),
            pltpu.VMEM((D, HEAD), F32),
            pltpu.VMEM((NZ, NC, PART, BLOCK), F32),
            pltpu.VMEM((NC, NZ, PART, BLOCK), F32),
            pltpu.VMEM((3, NZ * RANK, BLOCK), BF16),
            pltpu.VMEM((CHUNKS, NC, NZ * PART, WIDE), F32),
            pltpu.VMEM((CHUNKS, NZ * PART, WIDE), F32),
            pltpu.VMEM((CHUNKS, NX, NZ * PART, LANES), F32),
            pltpu.VMEM((CHUNKS, NX - 1, NZ * PART, LANES), F32),
            pltpu.VMEM((CHUNKS, NZ * PART, LANES), F32),
            pltpu.VMEM((NY - 1, NZ * PART, LANES), F32),
            pltpu.VMEM((NZ, PART, LANES), F32),
            pltpu.VMEM((NZ - 1, PART, LANES), F32),
            pltpu.VMEM((NC, NY, NX, PART, LANES), F32),
            pltpu.VMEM((CHUNKS, RANK, WIDE), F32),
            pltpu.VMEM((CHUNKS, RANK, WIDE), F32),
            pltpu.VMEM((D, 4 * RANK), BF16),
            pltpu.VMEM((RANK, HEAD), F32),
            pltpu.VMEM((2, RANK, HEAD), F32),
            pltpu.VMEM((NX, PART, HEAD), F32),
            pltpu.VMEM((NY, PART, HEAD), F32),
            pltpu.VMEM((NY, PART, HEAD), F32),
            pltpu.VMEM((NX, PART, HEAD), F32),
            dma((CHUNKS,)), dma, dma, dma,
            dma((2, 4, CHUNKS)), dma((2, 4, CHUNKS)),
            dma((NZ - 1,)), dma,
            dma((CHUNKS,)), dma((CHUNKS,)),
            dma((CHUNKS,)), dma((CHUNKS,)),
            dma((CHUNKS,)), dma,
            dma((NZ - 1,)), dma,
            dma((3,)), dma((3,)),
            dma((5,)), dma((5,)),
        ],
        compiler_params=pltpu.CompilerParams(
            collective_id=0, has_side_effects=True, vmem_limit_bytes=56 * 2**20
        ),
    )(acts, grad_out, error[0], q_init.T)
    return new_error[None], q_t.T, p_t.T[None]


def solution(mesh):
    return jax.shard_map(
        per_device,
        mesh=mesh,
        in_specs=(
            P(("dp", "tensor"), None),
            P("dp", "tensor"),
            P("dp", None, "tensor"),
            P("tensor", None),
        ),
        out_specs=(P("dp", None, "tensor"), P("tensor", None), P("tensor", None, None)),
        check_vma=False,
    )
```

```python
import jax
import jax.numpy as jnp
from jax import lax
from jax.experimental import pallas as pl
from jax.experimental.pallas import tpu as pltpu
from jax.sharding import PartitionSpec as P

NX, NY, NC, NZ = 4, 8, 2, 8
D, HEAD, RANK, TOK = 4096, 128, 32, 1024
BLOCK = TOK // NZ
CHUNKS = 8
AHEAD = 2
WIDE = D // CHUNKS
LANES = WIDE // NX
PART = RANK // NC
F32, BF16 = jnp.float32, jnp.bfloat16
HIGHEST = lax.Precision.HIGHEST
MESH = pl.DeviceIdType.MESH
NT = ((1,), (1,))
NN = ((1,), (0,))
TN = ((0,), (0,))


def exact(a, b, dims=NN):
    return lax.dot_general(a, b, (dims, ((), ())), precision=HIGHEST, preferred_element_type=F32)


def single(a, b, dims=NN):
    return lax.dot_general(a, b, (dims, ((), ())), preferred_element_type=F32)


def split(value, parts):
    out = []
    for _ in range(parts):
        out.append(value.astype(BF16))
        value = value - out[-1].astype(F32)
    return out


def inverse_factor(gram):
    n = RANK
    row = lax.broadcasted_iota(jnp.int32, (n, n), 0)
    col = lax.broadcasted_iota(jnp.int32, (n, n), 1)
    both = jnp.concatenate([gram, jnp.where(row == col, 1.0, 0.0).astype(F32)], axis=1)
    rows = lax.broadcasted_iota(jnp.int32, (n, 1), 0)
    for j in range(n):
        inv = 1.0 / jnp.sqrt(both[j : j + 1, j : j + 1])
        pivot = both[j : j + 1, :] * inv
        factor = both[:, j : j + 1] * inv
        both = jnp.where(rows > j, both - factor * pivot, jnp.where(rows == j, pivot, both))
    return both[:, n:]


def kernel(
    acts, grad_out, error, q_init,
    merged, pb_rows, q_out, p_out,
    abuf, gbuf, ebuf, qbuf,
    w_out, w_in, w_split, partial, core_in, core_sum, x_in, x_sum, y_in, y_sum, z_in,
    pg, pt, pb, small, q_acc, q_core, qx_a, qy_a, qy_b, qx_b,
    load_sem, g_sem, e_sem, i_sem, z_send, z_recv, w_send, w_recv,
    c_send, c_recv, x_send, x_recv, y_send, y_recv, s_send, s_recv, p_send, p_recv, q_send, q_recv,
):
    dp = lax.axis_index("dp")
    z = lax.axis_index("tensor")
    core = lax.rem(dp, NC)
    y = lax.rem(dp // NC, NY)
    x = dp // (NC * NY)

    def at(x_, y_, core_):
        return ((x_ * NY + y_) * NC + core_, z)

    sibling = at(x, y, 1 - core)
    ys = [at(x, lax.rem(y + k, NY), core) for k in range(1, NY)]
    xs = [at(lax.rem(x + k, NX), y, core) for k in range(1, NX)]
    zs = [(dp, lax.rem(z + k, NZ)) for k in range(1, NZ)]
    up, down = zs[0], zs[-1]

    def to(ref_from, ref_to, send_sem, recv_sem, device):
        return pltpu.make_async_remote_copy(
            src_ref=ref_from, dst_ref=ref_to, send_sem=send_sem, recv_sem=recv_sem,
            device_id=device, device_id_type=MESH,
        )

    def wait_bytes(ref, sem):
        pltpu.make_async_copy(ref, ref, sem).wait()

    def load(c):
        columns = pl.ds(pl.multiple_of(c * WIDE, WIDE), WIDE)
        return pltpu.make_async_copy(acts.at[:, columns], abuf.at[c, z], load_sem.at[c])

    load_q = pltpu.make_async_copy(q_init, qbuf, i_sem)
    load_g = pltpu.make_async_copy(grad_out, gbuf, g_sem)
    load_e = pltpu.make_async_copy(error, ebuf, e_sem)
    load_q.start()
    load_g.start()

    @pl.loop(0, CHUNKS)
    def _(c):
        load(c).start()

    load_e.start()

    barrier = pltpu.get_barrier_semaphore()
    partners = [sibling] + ys + xs + zs
    for device in partners:
        pl.semaphore_signal(barrier, inc=1, device_id=device, device_id_type=MESH)

    def z_copy(c, hop, way, sending):
        step = hop - 1 if sending else hop
        slot = lax.rem(z + (NZ - step if way == 0 else step), NZ)
        ref = abuf.at[c, slot]
        if hop == 4:
            ref = abuf.at[c, slot, pl.ds(way * (BLOCK // 2), BLOCK // 2)]
        source = ref
        if sending and hop == 1:
            source = acts.at[:, pl.ds(pl.multiple_of(c * WIDE, WIDE), WIDE)]
        return to(source, ref, z_send.at[way, hop - 1, c], z_recv.at[way, hop - 1, c], up if way == 0 else down)

    def own_send(c):
        for way in range(2):
            z_copy(c, 1, way, True).start()

    load_q.wait()
    load_g.wait()
    q_parts = jnp.concatenate(split(qbuf[...], 3), axis=0)
    w_all = single(q_parts, gbuf[...], NT)
    w_all = w_all[:RANK] + w_all[RANK : 2 * RANK] + w_all[2 * RANK :]
    for s in range(NZ):
        for h in range(NC):
            w_out[s, h] = w_all[h * PART : (h + 1) * PART, s * BLOCK : (s + 1) * BLOCK]

    pl.semaphore_wait(barrier, len(partners))

    def w_copy(k):
        return to(w_out.at[lax.rem(z + k, NZ)], w_in.at[:, z], w_send.at[k - 1], w_recv, zs[k - 1])

    for k in range(1, NZ):
        w_copy(k).start()
    w_in[:, z] = w_out[z]
    for c in range(AHEAD):
        own_send(c)

    @pl.loop(0, CHUNKS)
    def _(c):
        load(c).wait()


    def on(c, act):
        pl.when(jnp.logical_and(c >= 0, c < CHUNKS))(lambda: act(c))

    def forward(hop):
        def act(c):
            for way in range(2):
                z_copy(c, hop, way, False).wait_recv()
                z_copy(c, hop + 1, way, True).start()
        return act

    def rows_of(c):
        return pl.ds(pl.multiple_of(c * WIDE, WIDE), WIDE)

    def multiply(c):
        for way in range(2):
            z_copy(c, 4, way, False).wait_recv()
        grad = single(abuf[c].reshape(TOK, WIDE), gbuf[...], TN)
        merged[rows_of(c), :] = grad + ebuf[rows_of(c), :].astype(F32)

    def w_ready():
        wait_bytes(w_in.at[:, pl.ds(0, NZ - 1)], w_recv)
        load_e.wait()
        w = w_in[...].reshape(NZ * RANK, BLOCK)
        for part, value in enumerate(split(w, 3)):
            w_split[part] = value

    def core_copy(i):
        return to(partial.at[i, 1 - core], core_in.at[i], c_send.at[i], c_recv.at[i], sibling)

    def p_partial(i):
        c = lax.rem(y + 1 + i, CHUNKS)
        a = abuf[c, z]
        total = single(w_split[0], a) + (single(w_split[1], a) + single(w_split[2], a))
        partial[i] = total.reshape(NC, NZ * PART, WIDE)
        e_all = single(jnp.concatenate(split(qbuf[...], 3), axis=0), ebuf[rows_of(c), :], NT)
        e_all = e_all[:RANK] + (e_all[RANK : 2 * RANK] + e_all[2 * RANK :])
        mine = pl.ds(pl.multiple_of(z * PART, PART), PART)
        for h in range(NC):
            partial[i, h, mine, :] = partial[i, h, mine, :] + e_all[h * PART : (h + 1) * PART]
        core_copy(i).start()

    def p_core(i):
        core_copy(i).wait_recv()
        total = partial[i, core] + core_in[i]
        for j in range(NX):
            core_sum[i, j] = total[:, j * LANES : (j + 1) * LANES]
        for k in range(1, NX):
            to(core_sum.at[i, lax.rem(x + k, NX)], x_in.at[i, k - 1], x_send.at[i], x_recv.at[i], xs[k - 1]).start()

    def y_copy(i):
        device = at(x, lax.rem(y + 1 + i, NY), core)
        return to(x_sum.at[i], y_in.at[i], y_send.at[i], y_recv, device)

    def p_x(i):
        wait_bytes(x_in.at[i], x_recv.at[i])
        total = core_sum[i, x]
        for k in range(NX - 1):
            total = total + x_in[i, k]
        x_sum[i] = total
        pl.when(i < CHUNKS - 1)(lambda: y_copy(i).start())

    def s_copy(k):
        return to(y_sum.at[lax.rem(z + k, NZ)], z_in.at[k - 1], s_send.at[k - 1], s_recv, zs[k - 1])

    def p_y():
        wait_bytes(y_in, y_recv)
        total = x_sum[CHUNKS - 1]
        for k in range(NY - 1):
            total = total + y_in[k]
        y_sum[...] = total.reshape(NZ, PART, LANES)
        for k in range(1, NZ):
            s_copy(k).start()

    def p_z():
        wait_bytes(z_in, s_recv)
        total = y_sum[z]
        for k in range(NZ - 1):
            total = total + z_in[k]
        mine = pg.at[core, y, x]
        mine[...] = total
        for device in xs:
            to(mine, mine, p_send.at[0], p_recv.at[0], device).start()

    def gather_y():
        wait_bytes(pg.at[core, y, pl.ds(0, NX - 1)], p_recv.at[0])
        for device in ys:
            to(pg.at[core, y], pg.at[core, y], p_send.at[1], p_recv.at[1], device).start()

    def gather_core():
        wait_bytes(pg.at[core, pl.ds(0, NY - 1)], p_recv.at[1])
        to(pg.at[core], pg.at[core], p_send.at[2], p_recv.at[2], sibling).start()

    def gather_done():
        wait_bytes(pg.at[core], p_recv.at[2])

        @pl.loop(0, CHUNKS)
        def _(c):
            for h in range(NC):
                for j in range(NX):
                    pt[c, h * PART : (h + 1) * PART, j * LANES : (j + 1) * LANES] = pg[h, c, j]

    def make_gram():
        tall = pt[...].reshape(CHUNKS * RANK, WIDE)
        square = exact(tall, tall, NT)
        gram = square[:RANK, :RANK]
        for c in range(1, CHUNKS):
            gram = gram + square[c * RANK : (c + 1) * RANK, c * RANK : (c + 1) * RANK]
        small[...] = gram

    def make_inverse():
        small[...] = inverse_factor(small[...])

    def basis():
        inverse = small[...]
        wide = jnp.concatenate([jnp.concatenate([inverse] * CHUNKS, axis=0)] * CHUNKS, axis=1)
        group_r = lax.broadcasted_iota(jnp.int32, wide.shape, 0) // RANK
        group_c = lax.broadcasted_iota(jnp.int32, wide.shape, 1) // RANK
        blocks = jnp.where(group_r == group_c, wide, 0.0)
        pb[...] = exact(blocks, pt[...].reshape(CHUNKS * RANK, WIDE)).reshape(CHUNKS, RANK, WIDE)

    def basis_rows():
        @pl.loop(0, CHUNKS)
        def _(c):
            value = pb[c]
            p_out[:, rows_of(c)] = value
            high, low = [part.astype(F32) for part in split(value, 2)]
            stacked = jnp.concatenate([high, low, high, low], axis=0)
            pb_rows[rows_of(c), :] = stacked.T.astype(BF16)

        q_acc[...] = jnp.zeros_like(q_acc)

    def q_part(c):
        high, low = split(pb[c], 2)
        m_high, m_low = split(merged[rows_of(c), :], 2)
        first = single(jnp.concatenate([high, low], axis=0), m_high)
        q_acc[...] += first[:RANK] + (first[RANK:] + single(high, m_low))

    def q_early(start, end):
        @pl.loop(start, end)
        def _(c):
            q_part(c)

    def when(k, tick, *acts_):
        @pl.when(k == tick)
        def _():
            for act in acts_:
                act()

    @pl.loop(0, CHUNKS + 4)
    def _(k):
        on(k + AHEAD, own_send)
        step = 3 * k - 3
        when(k, 1, w_ready)
        on(step, p_partial)
        on(step - 2, p_x)
        when(k, 6, gather_y)
        when(k, 7, gather_done)
        when(k, 8, lambda: q_early(0, 3))
        on(k - 1, forward(1))
        on(step, p_core)
        on(step + 1, p_partial)
        on(step - 1, p_x)
        when(k, 4, p_y)
        when(k, 7, make_gram)
        when(k, 8, lambda: q_early(3, 4))
        on(k - 2, forward(2))
        on(step + 1, p_core)
        on(step + 2, p_partial)
        when(k, 5, p_z)
        when(k, 7, make_inverse)
        on(k - 3, forward(3))
        on(step + 2, p_core)
        on(step, p_x)
        when(k, 6, gather_core)
        when(k, 7, basis, basis_rows)
        on(k - 4, multiply)
        pl.when(k >= 8)(lambda: q_part(k - 4))

    q_core[0] = q_acc[...]
    q_c = to(q_core.at[0], q_core.at[1], q_send.at[0], q_recv.at[0], sibling)
    q_c.start()
    q_c.wait_recv()
    both = q_core[0] + q_core[1]

    def share(buf, place, value, sem, devices):
        buf[place] = value
        for device in devices:
            to(buf.at[place], buf.at[place], q_send.at[sem], q_recv.at[sem], device).start()

    def total_of(buf, sem):
        n = buf.shape[0]
        wait_bytes(buf.at[pl.ds(0, n - 1)], q_recv.at[sem])
        total = buf[0]
        for k in range(1, n):
            total = total + buf[k]
        return total

    share(qy_b, y, both[PART:], 2, ys)
    share(qx_a, x, both[:PART], 1, xs)
    share(qy_a, y, total_of(qx_a, 1), 3, ys)
    share(qx_b, x, total_of(qy_b, 2), 4, xs)
    q_t = jnp.concatenate([total_of(qy_a, 3), total_of(qx_b, 4)], axis=0)
    q_out[...] = q_t

    @pl.loop(0, CHUNKS)
    def _(c):
        for way in range(2):
            for hop in range(1, 5):
                z_copy(c, hop, way, True).wait_send()
        core_copy(c).wait_send()
        wait_bytes(x_in.at[c], x_send.at[c])
        pl.when(c < CHUNKS - 1)(lambda: y_copy(c).wait_send())

    for k in range(1, NZ):
        w_copy(k).wait_send()
        s_copy(k).wait_send()
    wait_bytes(pg.at[core, y, pl.ds(0, NX - 1)], p_send.at[0])
    wait_bytes(pg.at[core, pl.ds(0, NY - 1)], p_send.at[1])
    wait_bytes(pg.at[core], p_send.at[2])
    q_c.wait_send()
    wait_bytes(qx_a.at[pl.ds(0, NX - 1)], q_send.at[1])
    wait_bytes(qy_b.at[pl.ds(0, NY - 1)], q_send.at[2])
    wait_bytes(qy_a.at[pl.ds(0, NY - 1)], q_send.at[3])
    wait_bytes(qx_b.at[pl.ds(0, NX - 1)], q_send.at[4])


def update_kernel(merged, rows, q_t, p_t, new_error, q_out, p_out, buf, sems):
    save_q = pltpu.make_async_copy(q_t, q_out, sems.at[CHUNKS])
    save_p = pltpu.make_async_copy(p_t, p_out, sems.at[CHUNKS + 1])
    save_q.start()
    save_p.start()
    high, low = split(q_t[...] * (1.0 / (NX * NY * NC)), 2)
    back = jnp.concatenate([high, high, low, low], axis=0)

    def save(c):
        part = pl.ds(c * WIDE, WIDE)
        return pltpu.make_async_copy(buf.at[part], new_error.at[part], sems.at[c])

    for c in range(CHUNKS):
        part = pl.ds(c * WIDE, WIDE)
        buf[part, :] = (merged[part, :] - single(rows[part, :], back)).astype(BF16)
        save(c).start()
    for c in range(CHUNKS):
        save(c).wait()
    save_q.wait()
    save_p.wait()


def per_device(acts, grad_out, error, q_init):
    dma = pltpu.SemaphoreType.DMA
    hbm = pl.BlockSpec(memory_space=pltpu.HBM)
    vmem = pl.BlockSpec(memory_space=pltpu.VMEM)

    def stay(array, place):
        return pltpu.with_memory_space_constraint(array, place)

    merged, rows, q_t, p_t = pl.pallas_call(
        kernel,
        out_shape=(
            pltpu.VMEM((D, HEAD), F32),
            pltpu.VMEM((D, 4 * RANK), BF16),
            pltpu.VMEM((RANK, HEAD), F32),
            pltpu.VMEM((RANK, D), F32),
        ),
        in_specs=[hbm] * 4,
        out_specs=(vmem,) * 4,
        scratch_shapes=[
            pltpu.VMEM((CHUNKS, NZ, BLOCK, WIDE), BF16),
            pltpu.VMEM((TOK, HEAD), BF16),
            pltpu.VMEM((D, HEAD), BF16),
            pltpu.VMEM((RANK, HEAD), F32),
            pltpu.VMEM((NZ, NC, PART, BLOCK), F32),
            pltpu.VMEM((NC, NZ, PART, BLOCK), F32),
            pltpu.VMEM((3, NZ * RANK, BLOCK), BF16),
            pltpu.VMEM((CHUNKS, NC, NZ * PART, WIDE), F32),
            pltpu.VMEM((CHUNKS, NZ * PART, WIDE), F32),
            pltpu.VMEM((CHUNKS, NX, NZ * PART, LANES), F32),
            pltpu.VMEM((CHUNKS, NX - 1, NZ * PART, LANES), F32),
            pltpu.VMEM((CHUNKS, NZ * PART, LANES), F32),
            pltpu.VMEM((NY - 1, NZ * PART, LANES), F32),
            pltpu.VMEM((NZ, PART, LANES), F32),
            pltpu.VMEM((NZ - 1, PART, LANES), F32),
            pltpu.VMEM((NC, NY, NX, PART, LANES), F32),
            pltpu.VMEM((CHUNKS, RANK, WIDE), F32),
            pltpu.VMEM((CHUNKS, RANK, WIDE), F32),
            pltpu.VMEM((RANK, RANK), F32),
            pltpu.VMEM((RANK, HEAD), F32),
            pltpu.VMEM((2, RANK, HEAD), F32),
            pltpu.VMEM((NX, PART, HEAD), F32),
            pltpu.VMEM((NY, PART, HEAD), F32),
            pltpu.VMEM((NY, PART, HEAD), F32),
            pltpu.VMEM((NX, PART, HEAD), F32),
            dma((CHUNKS,)), dma, dma, dma,
            dma((2, 4, CHUNKS)), dma((2, 4, CHUNKS)),
            dma((NZ - 1,)), dma,
            dma((CHUNKS,)), dma((CHUNKS,)),
            dma((CHUNKS,)), dma((CHUNKS,)),
            dma((CHUNKS,)), dma,
            dma((NZ - 1,)), dma,
            dma((3,)), dma((3,)),
            dma((5,)), dma((5,)),
        ],
        compiler_params=pltpu.CompilerParams(
            collective_id=0, has_side_effects=True, vmem_limit_bytes=40 * 2**20
        ),
    )(*[stay(array, pltpu.HBM) for array in (acts, grad_out, error[0], q_init.T)])
    new_error, q_t, p_t = pl.pallas_call(
        update_kernel,
        out_shape=(
            jax.ShapeDtypeStruct((D, HEAD), BF16),
            jax.ShapeDtypeStruct((RANK, HEAD), F32),
            jax.ShapeDtypeStruct((RANK, D), F32),
        ),
        in_specs=[vmem] * 4,
        out_specs=(hbm,) * 3,
        scratch_shapes=[pltpu.VMEM((D, HEAD), BF16), dma((CHUNKS + 2,))],
        compiler_params=pltpu.CompilerParams(vmem_limit_bytes=40 * 2**20),
    )(*[stay(array, pltpu.VMEM) for array in (merged, rows, q_t, p_t)])
    return new_error[None], q_t.T, p_t.T[None]


def solution(mesh):
    return jax.shard_map(
        per_device,
        mesh=mesh,
        in_specs=(
            P(("dp", "tensor"), None),
            P("dp", "tensor"),
            P("dp", None, "tensor"),
            P("tensor", None),
        ),
        out_specs=(P("dp", None, "tensor"), P("tensor", None), P("tensor", None, None)),
        check_vma=False,
    )
```

```python
import jax
import jax.numpy as jnp
from jax import lax
from jax.experimental import pallas as pl
from jax.experimental.pallas import tpu as pltpu
from jax.sharding import PartitionSpec as P

NX, NY, NC, NZ = 4, 8, 2, 8
D, HEAD, RANK, TOK = 4096, 128, 32, 1024
BLOCK = TOK // NZ
CHUNKS = 8
AHEAD = 2
FAR = NZ // 2
WIDE = D // CHUNKS
LANES = WIDE // NX
PART = RANK // NC
F32, BF16 = jnp.float32, jnp.bfloat16
HIGHEST = lax.Precision.HIGHEST
MESH = pl.DeviceIdType.MESH
NT = ((1,), (1,))
NN = ((1,), (0,))
TN = ((0,), (0,))


def exact(a, b, dims=NN):
    return lax.dot_general(a, b, (dims, ((), ())), precision=HIGHEST, preferred_element_type=F32)


def single(a, b, dims=NN):
    return lax.dot_general(a, b, (dims, ((), ())), preferred_element_type=F32)


def split(value, parts):
    out = []
    for _ in range(parts):
        out.append(value.astype(BF16))
        value = value - out[-1].astype(F32)
    return out


def inverse_factor(gram):
    n = RANK
    row = lax.broadcasted_iota(jnp.int32, (n, n), 0)
    col = lax.broadcasted_iota(jnp.int32, (n, n), 1)
    both = jnp.concatenate([gram, jnp.where(row == col, 1.0, 0.0).astype(F32)], axis=1)
    rows = lax.broadcasted_iota(jnp.int32, (n, 1), 0)
    for j in range(n):
        inv = 1.0 / jnp.sqrt(both[j : j + 1, j : j + 1])
        pivot = both[j : j + 1, :] * inv
        factor = both[:, j : j + 1] * inv
        both = jnp.where(rows > j, both - factor * pivot, jnp.where(rows == j, pivot, both))
    return both[:, n:]


def kernel(
    acts, grad_out, error, q_init,
    merged, pb_rows, q_out, p_out,
    abuf, gbuf, ebuf, qbuf,
    w_out, w_in, w_split, partial, core_in, core_sum, x_in, x_sum, y_in, y_sum, z_in,
    gperm, pg, pt, pb, small, u_out, u_in, q_acc, q_core, qx_a, qy_a, qy_b, qx_b,
    load_sem, g_sem, e_sem, i_sem, z_send, z_recv, w_send, w_recv,
    c_send, c_recv, x_send, x_recv, y_send, y_recv, s_send, s_recv, p_send, p_recv, u_send, u_recv, q_send, q_recv,
):
    dp = lax.axis_index("dp")
    z = lax.axis_index("tensor")
    core = lax.rem(dp, NC)
    y = lax.rem(dp // NC, NY)
    x = dp // (NC * NY)

    def at(x_, y_, core_):
        return ((x_ * NY + y_) * NC + core_, z)

    sibling = at(x, y, 1 - core)
    ys = [at(x, lax.rem(y + k, NY), core) for k in range(1, NY)]
    xs = [at(lax.rem(x + k, NX), y, core) for k in range(1, NX)]
    zs = [(dp, lax.rem(z + k, NZ)) for k in range(1, NZ)]
    up, down = zs[0], zs[-1]

    def to(ref_from, ref_to, send_sem, recv_sem, device):
        return pltpu.make_async_remote_copy(
            src_ref=ref_from, dst_ref=ref_to, send_sem=send_sem, recv_sem=recv_sem,
            device_id=device, device_id_type=MESH,
        )

    def wait_bytes(ref, sem):
        pltpu.make_async_copy(ref, ref, sem).wait()

    def load(c):
        columns = pl.ds(pl.multiple_of(c * WIDE, WIDE), WIDE)
        return pltpu.make_async_copy(acts.at[:, columns], abuf.at[c, 0], load_sem.at[c])

    load_q = pltpu.make_async_copy(q_init, qbuf, i_sem)
    load_g = pltpu.make_async_copy(grad_out, gbuf, g_sem)
    load_e = pltpu.make_async_copy(error, ebuf, e_sem)
    load_q.start()
    load_g.start()

    @pl.loop(0, CHUNKS)
    def _(c):
        load(c).start()

    load_e.start()

    barrier = pltpu.get_barrier_semaphore()
    partners = [sibling] + ys + xs + zs
    for device in partners:
        pl.semaphore_signal(barrier, inc=1, device_id=device, device_id_type=MESH)

    def slot_of(hop, way):
        d = hop if way == 0 else (NZ - hop) % NZ
        return NZ - 1 if d == FAR else d - (d > FAR)

    def z_copy(c, hop, way):
        source = abuf.at[c, slot_of(hop - 1, way)]
        target = abuf.at[c, slot_of(hop, way)]
        if hop == FAR:
            part = pl.ds(way * (BLOCK // 2), BLOCK // 2)
            source, target = source.at[part], target.at[part]
        return to(source, target, z_send.at[way, hop - 1, c], z_recv.at[way, hop - 1, c], up if way == 0 else down)

    def own_send(c):
        for way in range(2):
            z_copy(c, 1, way).start()

    load_q.wait()
    load_g.wait()
    q_parts = jnp.concatenate(split(qbuf[...], 3), axis=0)
    w_all = single(q_parts, gbuf[...], NT)
    w_all = w_all[:RANK] + w_all[RANK : 2 * RANK] + w_all[2 * RANK :]
    for s in range(NZ):
        for h in range(NC):
            w_out[s, h] = w_all[h * PART : (h + 1) * PART, s * BLOCK : (s + 1) * BLOCK]

    @pl.loop(0, CHUNKS)
    def _(c):
        load(c).wait()

    pl.semaphore_wait(barrier, len(partners))

    def w_copy(k):
        return to(w_out.at[lax.rem(z + k, NZ)], w_in.at[:, z], w_send.at[k - 1], w_recv, zs[k - 1])

    for k in range(1, NZ):
        w_copy(k).start()
    w_in[:, z] = w_out[z]
    for c in range(AHEAD):
        own_send(c)

    for d in range(NZ):
        rows = pl.ds(pl.multiple_of(lax.rem(z + NZ - d, NZ) * BLOCK, BLOCK), BLOCK)
        place = NZ - 1 if d == FAR else d - (d > FAR)
        gperm[place] = gbuf[rows, :]


    def on(c, act):
        pl.when(jnp.logical_and(c >= 0, c < CHUNKS))(lambda: act(c))

    def forward(hop):
        def act(c):
            for way in range(2):
                z_copy(c, hop, way).wait_recv()
                z_copy(c, hop + 1, way).start()
        return act

    def rows_of(c):
        return pl.ds(pl.multiple_of(c * WIDE, WIDE), WIDE)

    def multiply(c):
        for way in range(2):
            z_copy(c, FAR - 1, way).wait_recv()
        near = NZ - 1
        grad = single(abuf[c, :near].reshape(near * BLOCK, WIDE), gperm[:near].reshape(near * BLOCK, HEAD), TN)
        merged[rows_of(c), :] = grad + ebuf[rows_of(c), :].astype(F32)

    def far_send(c):
        for way in range(2):
            z_copy(c, FAR, way).start()

    def finish(c):
        for way in range(2):
            z_copy(c, FAR, way).wait_recv()
        merged[rows_of(c), :] += single(abuf[c, NZ - 1], gperm[NZ - 1], TN)

    def w_ready():
        wait_bytes(w_in.at[:, pl.ds(0, NZ - 1)], w_recv)
        load_e.wait()
        w = w_in[...].reshape(NZ * RANK, BLOCK)
        for part, value in enumerate(split(w, 3)):
            w_split[part] = value

    def core_copy(i):
        return to(partial.at[i, 1 - core], core_in.at[i], c_send.at[i], c_recv.at[i], sibling)

    def p_partial(i):
        c = lax.rem(y + 1 + i, CHUNKS)
        a = abuf[c, 0]
        total = single(w_split[0], a) + (single(w_split[1], a) + single(w_split[2], a))
        partial[i] = total.reshape(NC, NZ * PART, WIDE)
        e_all = single(jnp.concatenate(split(qbuf[...], 3), axis=0), ebuf[rows_of(c), :], NT)
        e_all = e_all[:RANK] + (e_all[RANK : 2 * RANK] + e_all[2 * RANK :])
        mine = pl.ds(pl.multiple_of(z * PART, PART), PART)
        for h in range(NC):
            partial[i, h, mine, :] = partial[i, h, mine, :] + e_all[h * PART : (h + 1) * PART]
        core_copy(i).start()

    def p_core(i):
        core_copy(i).wait_recv()
        total = partial[i, core] + core_in[i]
        for j in range(NX):
            core_sum[i, j] = total[:, j * LANES : (j + 1) * LANES]
        for k in range(1, NX):
            to(core_sum.at[i, lax.rem(x + k, NX)], x_in.at[i, k - 1], x_send.at[i], x_recv.at[i], xs[k - 1]).start()

    def y_copy(i):
        device = at(x, lax.rem(y + 1 + i, NY), core)
        return to(x_sum.at[i], y_in.at[i], y_send.at[i], y_recv, device)

    def p_x(i):
        wait_bytes(x_in.at[i], x_recv.at[i])
        total = core_sum[i, x]
        for k in range(NX - 1):
            total = total + x_in[i, k]
        x_sum[i] = total
        pl.when(i < CHUNKS - 1)(lambda: y_copy(i).start())

    def s_copy(k, w):
        return to(y_sum.at[lax.rem(z + k + FAR * w, NZ)], z_in.at[w, k - 1], s_send.at[w, k - 1], s_recv.at[w], zs[k - 1])

    def p_y():
        wait_bytes(y_in, y_recv)
        total = x_sum[CHUNKS - 1]
        for k in range(NY - 1):
            total = total + y_in[k]
        y_sum[...] = total.reshape(NZ, PART, LANES)
        for k in range(1, NZ):
            for w in range(2):
                s_copy(k, w).start()

    def p_z():
        for w in range(2):
            wait_bytes(z_in.at[w], s_recv.at[w])
            total = y_sum[lax.rem(z + FAR * w, NZ)]
            for k in range(NZ - 1):
                total = total + z_in[w, k]
            mine = pg.at[w, core, x, y]
            mine[...] = total
            for device in ys:
                to(mine, mine, p_send.at[0, w], p_recv.at[0, w], device).start()

    def gather_x():
        for w in range(2):
            wait_bytes(pg.at[w, core, x, pl.ds(0, NY - 1)], p_recv.at[0, w])
            mine = pg.at[w, core, x]
            for device in xs:
                to(mine, mine, p_send.at[1, w], p_recv.at[1, w], device).start()

    def gather_core():
        for w in range(2):
            wait_bytes(pg.at[w, core, pl.ds(0, NX - 1)], p_recv.at[1, w])
            to(pg.at[w, core], pg.at[w, core], p_send.at[2, w], p_recv.at[2, w], sibling).start()

    def gather_done():
        for w in range(2):
            wait_bytes(pg.at[w, core], p_recv.at[2, w])

        @pl.loop(0, CHUNKS)
        def _(c):
            for w in range(2):
                for h in range(NC):
                    for j in range(NX):
                        pt[w, c, h * PART : (h + 1) * PART, j * LANES : (j + 1) * LANES] = pg[w, h, j, c]

    def u_copy():
        return to(u_out, u_in, u_send, u_recv, zs[FAR - 1])

    def three(stacked):
        return stacked[:RANK] + (stacked[RANK : 2 * RANK] + stacked[2 * RANK :])

    def u_make():
        u_out[...] = jnp.zeros_like(u_out)

        @pl.loop(0, CHUNKS)
        def _(c):
            u_out[...] += three(single(jnp.concatenate(split(pt[1, c], 3), axis=0), abuf[c, 0], NT))

        u_copy().start()

    def u_use():
        u_copy().wait_recv()
        far = three(single(jnp.concatenate(split(u_in[...], 3), axis=0), gperm[NZ - 1]))
        q_acc[...] += exact(small[...], far)

    def make_gram():
        tall = pt[0].reshape(CHUNKS * RANK, WIDE)
        square = exact(tall, tall, NT)
        gram = square[:RANK, :RANK]
        for c in range(1, CHUNKS):
            gram = gram + square[c * RANK : (c + 1) * RANK, c * RANK : (c + 1) * RANK]
        small[...] = gram

    def make_inverse():
        small[...] = inverse_factor(small[...])

    def basis():
        inverse = small[...]
        wide = jnp.concatenate([jnp.concatenate([inverse] * CHUNKS, axis=0)] * CHUNKS, axis=1)
        group_r = lax.broadcasted_iota(jnp.int32, wide.shape, 0) // RANK
        group_c = lax.broadcasted_iota(jnp.int32, wide.shape, 1) // RANK
        blocks = jnp.where(group_r == group_c, wide, 0.0)
        pb[...] = exact(blocks, pt[0].reshape(CHUNKS * RANK, WIDE)).reshape(CHUNKS, RANK, WIDE)

    def basis_rows():
        @pl.loop(0, CHUNKS)
        def _(c):
            value = pb[c]
            p_out[:, rows_of(c)] = value
            high, low = [part.astype(F32) for part in split(value, 2)]
            stacked = jnp.concatenate([high, low, high, low], axis=0)
            pb_rows[rows_of(c), :] = stacked.T.astype(BF16)

        q_acc[...] = jnp.zeros_like(q_acc)

    def q_part(c):
        high, low = split(pb[c], 2)
        m_high, m_low = split(merged[rows_of(c), :], 2)
        first = single(jnp.concatenate([high, low], axis=0), m_high)
        q_acc[...] += first[:RANK] + (first[RANK:] + single(high, m_low))

    def q_early(start, end):
        @pl.loop(start, end)
        def _(c):
            q_part(c)

    def when(k, tick, *acts_):
        @pl.when(k == tick)
        def _():
            for act in acts_:
                act()

    @pl.loop(0, CHUNKS + 3)
    def _(k):
        on(k + AHEAD, own_send)
        step = 3 * k - 3
        when(k, 1, w_ready)
        on(step, p_partial)
        on(step - 2, p_x)
        when(k, 8, basis, basis_rows)
        when(k, 9, u_use)
        on(k - 1, forward(1))
        on(step, p_core)
        on(step + 1, p_partial)
        on(step - 1, p_x)
        when(k, 6, gather_x)
        when(k, 7, gather_core)
        when(k, 8, lambda: q_early(0, 3))
        on(k - 2, forward(2))
        when(k, 8, lambda: far_send(0), lambda: far_send(1))
        when(k, 9, lambda: far_send(2), lambda: far_send(3), lambda: far_send(4), lambda: far_send(5))
        on(step + 1, p_core)
        on(step + 2, p_partial)
        when(k, 4, p_y)
        when(k, 5, p_z)
        when(k, 7, gather_done, u_make, make_gram)
        when(k, 8, lambda: q_early(3, 5))
        on(k - 3, multiply)
        on(step + 2, p_core)
        on(step, p_x)
        when(k, 7, make_inverse)
        pl.when(k >= 8)(lambda: q_part(k - 3))

    far_send(6)
    far_send(7)

    q_core[0] = q_acc[...]
    q_c = to(q_core.at[0], q_core.at[1], q_send.at[0], q_recv.at[0], sibling)
    q_c.start()

    def share(buf, place, value, sem, devices):
        buf[place] = value
        for device in devices:
            to(buf.at[place], buf.at[place], q_send.at[sem], q_recv.at[sem], device).start()

    def total_of(buf, sem):
        n = buf.shape[0]
        wait_bytes(buf.at[pl.ds(0, n - 1)], q_recv.at[sem])
        total = buf[0]
        for k in range(1, n):
            total = total + buf[k]
        return total

    finish(0)
    q_c.wait_recv()
    both = q_core[0] + q_core[1]
    share(qy_b, y, both[PART:], 2, ys)
    share(qx_a, x, both[:PART], 1, xs)
    finish(1)
    finish(2)
    share(qy_a, y, total_of(qx_a, 1), 3, ys)
    finish(3)
    share(qx_b, x, total_of(qy_b, 2), 4, xs)
    finish(4)
    finish(5)
    finish(6)
    q_out[...] = jnp.concatenate([total_of(qy_a, 3), total_of(qx_b, 4)], axis=0)
    finish(7)

    @pl.loop(0, CHUNKS)
    def _(c):
        for way in range(2):
            for hop in range(1, 5):
                z_copy(c, hop, way).wait_send()
        core_copy(c).wait_send()
        wait_bytes(x_in.at[c], x_send.at[c])
        pl.when(c < CHUNKS - 1)(lambda: y_copy(c).wait_send())

    for k in range(1, NZ):
        w_copy(k).wait_send()
        for w in range(2):
            s_copy(k, w).wait_send()
    for w in range(2):
        wait_bytes(pg.at[w, core, x, pl.ds(0, NY - 1)], p_send.at[0, w])
        wait_bytes(pg.at[w, core, pl.ds(0, NX - 1)], p_send.at[1, w])
        wait_bytes(pg.at[w, core], p_send.at[2, w])
    u_copy().wait_send()
    q_c.wait_send()
    wait_bytes(qx_a.at[pl.ds(0, NX - 1)], q_send.at[1])
    wait_bytes(qy_b.at[pl.ds(0, NY - 1)], q_send.at[2])
    wait_bytes(qy_a.at[pl.ds(0, NY - 1)], q_send.at[3])
    wait_bytes(qx_b.at[pl.ds(0, NX - 1)], q_send.at[4])


def update_kernel(merged, rows, q_t, p_t, new_error, q_out, p_out, buf, sems):
    save_q = pltpu.make_async_copy(q_t, q_out, sems.at[CHUNKS])
    save_p = pltpu.make_async_copy(p_t, p_out, sems.at[CHUNKS + 1])
    save_q.start()
    save_p.start()
    high, low = split(q_t[...] * (1.0 / (NX * NY * NC)), 2)
    back = jnp.concatenate([high, high, low, low], axis=0)

    def save(c):
        part = pl.ds(c * WIDE, WIDE)
        return pltpu.make_async_copy(buf.at[part], new_error.at[part], sems.at[c])

    for c in range(CHUNKS):
        part = pl.ds(c * WIDE, WIDE)
        buf[part, :] = (merged[part, :] - single(rows[part, :], back)).astype(BF16)
        save(c).start()
    for c in range(CHUNKS):
        save(c).wait()
    save_q.wait()
    save_p.wait()


def per_device(acts, grad_out, error, q_init):
    dma = pltpu.SemaphoreType.DMA
    hbm = pl.BlockSpec(memory_space=pltpu.HBM)
    vmem = pl.BlockSpec(memory_space=pltpu.VMEM)

    def stay(array, place):
        return pltpu.with_memory_space_constraint(array, place)

    merged, rows, q_t, p_t = pl.pallas_call(
        kernel,
        out_shape=(
            pltpu.VMEM((D, HEAD), F32),
            pltpu.VMEM((D, 4 * RANK), BF16),
            pltpu.VMEM((RANK, HEAD), F32),
            pltpu.VMEM((RANK, D), F32),
        ),
        in_specs=[hbm] * 4,
        out_specs=(vmem,) * 4,
        scratch_shapes=[
            pltpu.VMEM((CHUNKS, NZ, BLOCK, WIDE), BF16),
            pltpu.VMEM((TOK, HEAD), BF16),
            pltpu.VMEM((D, HEAD), BF16),
            pltpu.VMEM((RANK, HEAD), F32),
            pltpu.VMEM((NZ, NC, PART, BLOCK), F32),
            pltpu.VMEM((NC, NZ, PART, BLOCK), F32),
            pltpu.VMEM((3, NZ * RANK, BLOCK), BF16),
            pltpu.VMEM((CHUNKS, NC, NZ * PART, WIDE), F32),
            pltpu.VMEM((CHUNKS, NZ * PART, WIDE), F32),
            pltpu.VMEM((CHUNKS, NX, NZ * PART, LANES), F32),
            pltpu.VMEM((CHUNKS, NX - 1, NZ * PART, LANES), F32),
            pltpu.VMEM((CHUNKS, NZ * PART, LANES), F32),
            pltpu.VMEM((NY - 1, NZ * PART, LANES), F32),
            pltpu.VMEM((NZ, PART, LANES), F32),
            pltpu.VMEM((2, NZ - 1, PART, LANES), F32),
            pltpu.VMEM((NZ, BLOCK, HEAD), BF16),
            pltpu.VMEM((2, NC, NX, NY, PART, LANES), F32),
            pltpu.VMEM((2, CHUNKS, RANK, WIDE), F32),
            pltpu.VMEM((CHUNKS, RANK, WIDE), F32),
            pltpu.VMEM((RANK, RANK), F32),
            pltpu.VMEM((RANK, BLOCK), F32),
            pltpu.VMEM((RANK, BLOCK), F32),
            pltpu.VMEM((RANK, HEAD), F32),
            pltpu.VMEM((2, RANK, HEAD), F32),
            pltpu.VMEM((NX, PART, HEAD), F32),
            pltpu.VMEM((NY, PART, HEAD), F32),
            pltpu.VMEM((NY, PART, HEAD), F32),
            pltpu.VMEM((NX, PART, HEAD), F32),
            dma((CHUNKS,)), dma, dma, dma,
            dma((2, 4, CHUNKS)), dma((2, 4, CHUNKS)),
            dma((NZ - 1,)), dma,
            dma((CHUNKS,)), dma((CHUNKS,)),
            dma((CHUNKS,)), dma((CHUNKS,)),
            dma((CHUNKS,)), dma,
            dma((2, NZ - 1)), dma((2,)),
            dma((3, 2)), dma((3, 2)),
            dma, dma,
            dma((5,)), dma((5,)),
        ],
        compiler_params=pltpu.CompilerParams(
            collective_id=0, has_side_effects=True, vmem_limit_bytes=40 * 2**20
        ),
    )(*[stay(array, pltpu.HBM) for array in (acts, grad_out, error[0], q_init.T)])
    new_error, q_t, p_t = pl.pallas_call(
        update_kernel,
        out_shape=(
            jax.ShapeDtypeStruct((D, HEAD), BF16),
            jax.ShapeDtypeStruct((RANK, HEAD), F32),
            jax.ShapeDtypeStruct((RANK, D), F32),
        ),
        in_specs=[vmem] * 4,
        out_specs=(hbm,) * 3,
        scratch_shapes=[pltpu.VMEM((D, HEAD), BF16), dma((CHUNKS + 2,))],
        compiler_params=pltpu.CompilerParams(vmem_limit_bytes=40 * 2**20),
    )(*[stay(array, pltpu.VMEM) for array in (merged, rows, q_t, p_t)])
    return new_error[None], q_t.T, p_t.T[None]


def solution(mesh):
    return jax.shard_map(
        per_device,
        mesh=mesh,
        in_specs=(
            P(("dp", "tensor"), None),
            P("dp", "tensor"),
            P("dp", None, "tensor"),
            P("tensor", None),
        ),
        out_specs=(P("dp", None, "tensor"), P("tensor", None), P("tensor", None, None)),
        check_vma=False,
    )
```

```python
import jax
import jax.numpy as jnp
from jax import lax
from jax.experimental import pallas as pl
from jax.experimental.pallas import tpu as pltpu
from jax.sharding import PartitionSpec as P

NX, NY, NC, NZ = 4, 8, 2, 8
D, HEAD, RANK, TOK = 4096, 128, 32, 1024
BLOCK = TOK // NZ
CHUNKS = 8
AHEAD = 2
FAR = NZ // 2
WIDE = D // CHUNKS
LANES = WIDE // NX
PART = RANK // NC
F32, BF16 = jnp.float32, jnp.bfloat16
HIGHEST = lax.Precision.HIGHEST
MESH = pl.DeviceIdType.MESH
NT = ((1,), (1,))
NN = ((1,), (0,))
TN = ((0,), (0,))


def exact(a, b, dims=NN):
    return lax.dot_general(a, b, (dims, ((), ())), precision=HIGHEST, preferred_element_type=F32)


def single(a, b, dims=NN):
    return lax.dot_general(a, b, (dims, ((), ())), preferred_element_type=F32)


def split(value, parts):
    out = []
    for _ in range(parts):
        out.append(value.astype(BF16))
        value = value - out[-1].astype(F32)
    return out


def inverse_factor(gram):
    n = RANK
    row = lax.broadcasted_iota(jnp.int32, (n, n), 0)
    col = lax.broadcasted_iota(jnp.int32, (n, n), 1)
    both = jnp.concatenate([gram, jnp.where(row == col, 1.0, 0.0).astype(F32)], axis=1)
    rows = lax.broadcasted_iota(jnp.int32, (n, 1), 0)
    for j in range(n):
        inv = 1.0 / jnp.sqrt(both[j : j + 1, j : j + 1])
        pivot = both[j : j + 1, :] * inv
        factor = both[:, j : j + 1] * inv
        both = jnp.where(rows > j, both - factor * pivot, jnp.where(rows == j, pivot, both))
    return both[:, n:]


def kernel(
    acts, grad_out, error, q_init,
    merged, pb_rows, q_out, p_out,
    abuf, gbuf, ebuf, qbuf,
    w_out, w_in, w_split, partial, core_in, core_sum, x_in, x_sum, y_in, y_sum, z_in,
    gperm, pg, pt, pb, small, u_out, u_in, q_acc, q_core, qx_a, qy_a, qy_b, qx_b,
    load_sem, g_sem, e_sem, i_sem, z_send, z_recv, w_send, w_recv,
    c_send, c_recv, x_send, x_recv, y_send, y_recv, s_send, s_recv, p_send, p_recv, u_send, u_recv, q_send, q_recv,
):
    dp = lax.axis_index("dp")
    z = lax.axis_index("tensor")
    core = lax.rem(dp, NC)
    y = lax.rem(dp // NC, NY)
    x = dp // (NC * NY)

    def at(x_, y_, core_):
        return ((x_ * NY + y_) * NC + core_, z)

    sibling = at(x, y, 1 - core)
    ys = [at(x, lax.rem(y + k, NY), core) for k in range(1, NY)]
    xs = [at(lax.rem(x + k, NX), y, core) for k in range(1, NX)]
    zs = [(dp, lax.rem(z + k, NZ)) for k in range(1, NZ)]
    up, down = zs[0], zs[-1]

    def to(ref_from, ref_to, send_sem, recv_sem, device):
        return pltpu.make_async_remote_copy(
            src_ref=ref_from, dst_ref=ref_to, send_sem=send_sem, recv_sem=recv_sem,
            device_id=device, device_id_type=MESH,
        )

    def wait_bytes(ref, sem):
        pltpu.make_async_copy(ref, ref, sem).wait()

    def load(c):
        columns = pl.ds(pl.multiple_of(c * WIDE, WIDE), WIDE)
        return pltpu.make_async_copy(acts.at[:, columns], abuf.at[c, 0], load_sem.at[c])

    load_q = pltpu.make_async_copy(q_init, qbuf, i_sem)
    load_g = pltpu.make_async_copy(grad_out, gbuf, g_sem)
    load_e = pltpu.make_async_copy(error, ebuf, e_sem)
    load_q.start()
    load_g.start()

    @pl.loop(0, CHUNKS)
    def _(c):
        load(c).start()

    load_e.start()

    barrier = pltpu.get_barrier_semaphore()
    partners = [sibling] + ys + xs + zs
    for device in partners:
        pl.semaphore_signal(barrier, inc=1, device_id=device, device_id_type=MESH)

    def slot_of(hop, way):
        d = hop if way == 0 else (NZ - hop) % NZ
        return NZ - 1 if d == FAR else d - (d > FAR)

    def z_copy(c, hop, way):
        source = abuf.at[c, slot_of(hop - 1, way)]
        target = abuf.at[c, slot_of(hop, way)]
        if hop == FAR:
            part = pl.ds(way * (BLOCK // 2), BLOCK // 2)
            source, target = source.at[part], target.at[part]
        return to(source, target, z_send.at[way, hop - 1], z_recv.at[way, hop - 1, c], up if way == 0 else down)

    def own_send(c):
        for way in range(2):
            z_copy(c, 1, way).start()

    load_q.wait()
    load_g.wait()
    q_parts = jnp.concatenate(split(qbuf[...], 3), axis=0)
    w_all = single(q_parts, gbuf[...], NT)
    w_all = w_all[:RANK] + w_all[RANK : 2 * RANK] + w_all[2 * RANK :]
    for s in range(NZ):
        for h in range(NC):
            w_out[s, h] = w_all[h * PART : (h + 1) * PART, s * BLOCK : (s + 1) * BLOCK]

    @pl.loop(0, CHUNKS)
    def _(c):
        load(c).wait()

    pl.semaphore_wait(barrier, len(partners))

    def w_copy(k):
        return to(w_out.at[lax.rem(z + k, NZ)], w_in.at[:, z], w_send, w_recv, zs[k - 1])

    for k in range(1, NZ):
        w_copy(k).start()
    w_in[:, z] = w_out[z]
    for c in range(AHEAD):
        own_send(c)

    for d in range(NZ):
        rows = pl.ds(pl.multiple_of(lax.rem(z + NZ - d, NZ) * BLOCK, BLOCK), BLOCK)
        place = NZ - 1 if d == FAR else d - (d > FAR)
        gperm[place] = gbuf[rows, :]


    def on(c, act):
        pl.when(jnp.logical_and(c >= 0, c < CHUNKS))(lambda: act(c))

    def forward(hop):
        def act(c):
            for way in range(2):
                z_copy(c, hop, way).wait_recv()
                z_copy(c, hop + 1, way).start()
        return act

    def rows_of(c):
        return pl.ds(pl.multiple_of(c * WIDE, WIDE), WIDE)

    def multiply(c):
        for way in range(2):
            z_copy(c, FAR - 1, way).wait_recv()
        near = NZ - 1
        grad = single(abuf[c, :near].reshape(near * BLOCK, WIDE), gperm[:near].reshape(near * BLOCK, HEAD), TN)
        merged[rows_of(c), :] = grad + ebuf[rows_of(c), :].astype(F32)

    def far_send(c):
        for way in range(2):
            z_copy(c, FAR, way).start()

    def finish(c):
        for way in range(2):
            z_copy(c, FAR, way).wait_recv()
        merged[rows_of(c), :] += single(abuf[c, NZ - 1], gperm[NZ - 1], TN)

    def w_ready():
        wait_bytes(w_in.at[:, pl.ds(0, NZ - 1)], w_recv)
        load_e.wait()
        w = w_in[...].reshape(NZ * RANK, BLOCK)
        for part, value in enumerate(split(w, 3)):
            w_split[part] = value

    def core_copy(i):
        return to(partial.at[i, 1 - core], core_in.at[i], c_send, c_recv.at[i], sibling)

    def p_partial(i):
        c = lax.rem(y + 1 + i, CHUNKS)
        a = abuf[c, 0]
        total = single(w_split[0], a) + (single(w_split[1], a) + single(w_split[2], a))
        partial[i] = total.reshape(NC, NZ * PART, WIDE)
        e_all = single(jnp.concatenate(split(qbuf[...], 3), axis=0), ebuf[rows_of(c), :], NT)
        e_all = e_all[:RANK] + (e_all[RANK : 2 * RANK] + e_all[2 * RANK :])
        mine = pl.ds(pl.multiple_of(z * PART, PART), PART)
        for h in range(NC):
            partial[i, h, mine, :] = partial[i, h, mine, :] + e_all[h * PART : (h + 1) * PART]
        core_copy(i).start()

    def p_core(i):
        core_copy(i).wait_recv()
        total = partial[i, core] + core_in[i]
        for j in range(NX):
            core_sum[i, j] = total[:, j * LANES : (j + 1) * LANES]
        for k in range(1, NX):
            to(core_sum.at[i, lax.rem(x + k, NX)], x_in.at[i, k - 1], x_send, x_recv.at[i], xs[k - 1]).start()

    def y_copy(i):
        device = at(x, lax.rem(y + 1 + i, NY), core)
        return to(x_sum.at[i], y_in.at[i], y_send, y_recv, device)

    def p_x(i):
        wait_bytes(x_in.at[i], x_recv.at[i])
        total = core_sum[i, x]
        for k in range(NX - 1):
            total = total + x_in[i, k]
        x_sum[i] = total
        pl.when(i < CHUNKS - 1)(lambda: y_copy(i).start())

    def s_copy(k, w):
        return to(y_sum.at[lax.rem(z + k + FAR * w, NZ)], z_in.at[w, k - 1], s_send, s_recv.at[w], zs[k - 1])

    def p_y():
        wait_bytes(y_in, y_recv)
        total = x_sum[CHUNKS - 1]
        for k in range(NY - 1):
            total = total + y_in[k]
        y_sum[...] = total.reshape(NZ, PART, LANES)
        for k in range(1, NZ):
            for w in range(2):
                s_copy(k, w).start()

    def p_z():
        for w in range(2):
            wait_bytes(z_in.at[w], s_recv.at[w])
            total = y_sum[lax.rem(z + FAR * w, NZ)]
            for k in range(NZ - 1):
                total = total + z_in[w, k]
            mine = pg.at[w, core, x, y]
            mine[...] = total
            for device in ys:
                to(mine, mine, p_send.at[0, w], p_recv.at[0, w], device).start()

    def gather_x():
        for w in range(2):
            wait_bytes(pg.at[w, core, x, pl.ds(0, NY - 1)], p_recv.at[0, w])
            mine = pg.at[w, core, x]
            for device in xs:
                to(mine, mine, p_send.at[1, w], p_recv.at[1, w], device).start()

    def gather_core():
        for w in range(2):
            wait_bytes(pg.at[w, core, pl.ds(0, NX - 1)], p_recv.at[1, w])
            to(pg.at[w, core], pg.at[w, core], p_send.at[2, w], p_recv.at[2, w], sibling).start()

    def gather_done():
        for w in range(2):
            wait_bytes(pg.at[w, core], p_recv.at[2, w])

        @pl.loop(0, CHUNKS)
        def _(c):
            for w in range(2):
                for h in range(NC):
                    for j in range(NX):
                        pt[w, c, h * PART : (h + 1) * PART, j * LANES : (j + 1) * LANES] = pg[w, h, j, c]

    def u_copy():
        return to(u_out, u_in, u_send, u_recv, zs[FAR - 1])

    def three(stacked):
        return stacked[:RANK] + (stacked[RANK : 2 * RANK] + stacked[2 * RANK :])

    def u_make():
        u_out[...] = jnp.zeros_like(u_out)
        q_acc[...] = jnp.zeros_like(q_acc)

        @pl.loop(0, CHUNKS)
        def _(c):
            u_out[...] += three(single(jnp.concatenate(split(pt[1, c], 3), axis=0), abuf[c, 0], NT))

        u_copy().start()

    def u_use():
        u_copy().wait_recv()
        q_acc[...] += three(single(jnp.concatenate(split(u_in[...], 3), axis=0), gperm[NZ - 1]))

    def make_gram():
        tall = pt[0].reshape(CHUNKS * RANK, WIDE)
        square = exact(tall, tall, NT)
        gram = square[:RANK, :RANK]
        for c in range(1, CHUNKS):
            gram = gram + square[c * RANK : (c + 1) * RANK, c * RANK : (c + 1) * RANK]
        small[...] = gram

    def make_inverse():
        small[...] = inverse_factor(small[...])

    def basis():
        inverse = small[...]
        wide = jnp.concatenate([jnp.concatenate([inverse] * CHUNKS, axis=0)] * CHUNKS, axis=1)
        group_r = lax.broadcasted_iota(jnp.int32, wide.shape, 0) // RANK
        group_c = lax.broadcasted_iota(jnp.int32, wide.shape, 1) // RANK
        blocks = jnp.where(group_r == group_c, wide, 0.0)
        pb[...] = exact(blocks, pt[0].reshape(CHUNKS * RANK, WIDE)).reshape(CHUNKS, RANK, WIDE)

    def basis_rows():
        @pl.loop(0, CHUNKS)
        def _(c):
            value = pb[c]
            p_out[:, rows_of(c)] = value
            high, low = [part.astype(F32) for part in split(value, 2)]
            stacked = jnp.concatenate([high, low, high, low], axis=0)
            pb_rows[rows_of(c), :] = stacked.T.astype(BF16)

    def q_part(c):
        a = split(pt[0, c], 3)
        b = split(merged[rows_of(c), :], 3)
        first = three(single(jnp.concatenate(a, axis=0), b[0]))
        second = single(jnp.concatenate(a[:2], axis=0), b[1])
        q_acc[...] += first + (second[:RANK] + (second[RANK:] + single(a[0], b[2])))

    def q_early(start, end):
        @pl.loop(start, end)
        def _(c):
            q_part(c)

    def when(k, tick, *acts_):
        @pl.when(k == tick)
        def _():
            for act in acts_:
                act()

    @pl.loop(0, CHUNKS + 3)
    def _(k):
        on(k + AHEAD, own_send)
        step = 3 * k - 3
        when(k, 1, w_ready)
        on(step, p_partial)
        on(step - 2, p_x)
        on(k - 1, forward(1))
        on(step, p_core)
        on(step + 1, p_partial)
        on(step - 1, p_x)
        when(k, 8, gather_core)
        on(k - 2, forward(2))
        when(k, 9, *[lambda c=c: far_send(c) for c in range(6)])
        on(step + 1, p_core)
        on(step + 2, p_partial)
        when(k, 4, p_y)
        when(k, 5, p_z)
        when(k, 6, gather_x)
        when(k, 8, gather_done, u_make, lambda: q_early(0, 5))
        on(k - 3, multiply)
        on(step + 2, p_core)
        on(step, p_x)
        pl.when(k >= 8)(lambda: q_part(k - 3))

    u_use()
    far_send(6)
    far_send(7)

    q_core[0] = q_acc[...]
    q_c = to(q_core.at[0], q_core.at[1], q_send.at[0], q_recv.at[0], sibling)
    q_c.start()

    def share(buf, place, value, sem, devices):
        buf[place] = value
        for device in devices:
            to(buf.at[place], buf.at[place], q_send.at[sem], q_recv.at[sem], device).start()

    def total_of(buf, sem):
        n = buf.shape[0]
        wait_bytes(buf.at[pl.ds(0, n - 1)], q_recv.at[sem])
        total = buf[0]
        for k in range(1, n):
            total = total + buf[k]
        return total

    make_gram()
    q_c.wait_recv()
    both = q_core[0] + q_core[1]
    share(qy_b, y, both[PART:], 2, ys)
    share(qx_a, x, both[:PART], 1, xs)
    make_inverse()
    share(qy_a, y, total_of(qx_a, 1), 3, ys)
    basis()
    finish(0)
    share(qx_b, x, total_of(qy_b, 2), 4, xs)
    basis_rows()
    for c in range(1, CHUNKS - 1):
        finish(c)
    q_out[...] = exact(small[...], jnp.concatenate([total_of(qy_a, 3), total_of(qx_b, 4)], axis=0))
    finish(CHUNKS - 1)

    for way in range(2):
        for hop in range(1, FAR):
            wait_bytes(abuf.at[:, 0], z_send.at[way, hop - 1])
        wait_bytes(abuf.at[:, 0, pl.ds(0, BLOCK // 2)], z_send.at[way, FAR - 1])
    wait_bytes(w_in.at[:, pl.ds(0, NZ - 1)], w_send)
    wait_bytes(core_in, c_send)
    wait_bytes(x_in, x_send)
    wait_bytes(y_in, y_send)
    wait_bytes(z_in, s_send)
    for w in range(2):
        wait_bytes(pg.at[w, core, x, pl.ds(0, NY - 1)], p_send.at[0, w])
        wait_bytes(pg.at[w, core, pl.ds(0, NX - 1)], p_send.at[1, w])
        wait_bytes(pg.at[w, core], p_send.at[2, w])
    u_copy().wait_send()
    q_c.wait_send()
    wait_bytes(qx_a.at[pl.ds(0, NX - 1)], q_send.at[1])
    wait_bytes(qy_b.at[pl.ds(0, NY - 1)], q_send.at[2])
    wait_bytes(qy_a.at[pl.ds(0, NY - 1)], q_send.at[3])
    wait_bytes(qx_b.at[pl.ds(0, NX - 1)], q_send.at[4])


def update_kernel(merged, rows, q_t, p_t, new_error, q_out, p_out, buf, sems):
    save_q = pltpu.make_async_copy(q_t, q_out, sems.at[CHUNKS])
    save_p = pltpu.make_async_copy(p_t, p_out, sems.at[CHUNKS + 1])
    save_q.start()
    save_p.start()
    high, low = split(q_t[...] * (1.0 / (NX * NY * NC)), 2)
    back = jnp.concatenate([high, high, low, low], axis=0)

    def save(c):
        part = pl.ds(c * WIDE, WIDE)
        return pltpu.make_async_copy(buf.at[part], new_error.at[part], sems.at[c])

    for c in range(CHUNKS):
        part = pl.ds(c * WIDE, WIDE)
        buf[part, :] = (merged[part, :] - single(rows[part, :], back)).astype(BF16)
        save(c).start()
    for c in range(CHUNKS):
        save(c).wait()
    save_q.wait()
    save_p.wait()


def per_device(acts, grad_out, error, q_init):
    dma = pltpu.SemaphoreType.DMA
    hbm = pl.BlockSpec(memory_space=pltpu.HBM)
    vmem = pl.BlockSpec(memory_space=pltpu.VMEM)

    def stay(array, place):
        return pltpu.with_memory_space_constraint(array, place)

    merged, rows, q_t, p_t = pl.pallas_call(
        kernel,
        out_shape=(
            pltpu.VMEM((D, HEAD), F32),
            pltpu.VMEM((D, 4 * RANK), BF16),
            pltpu.VMEM((RANK, HEAD), F32),
            pltpu.VMEM((RANK, D), F32),
        ),
        in_specs=[hbm] * 4,
        out_specs=(vmem,) * 4,
        scratch_shapes=[
            pltpu.VMEM((CHUNKS, NZ, BLOCK, WIDE), BF16),
            pltpu.VMEM((TOK, HEAD), BF16),
            pltpu.VMEM((D, HEAD), BF16),
            pltpu.VMEM((RANK, HEAD), F32),
            pltpu.VMEM((NZ, NC, PART, BLOCK), F32),
            pltpu.VMEM((NC, NZ, PART, BLOCK), F32),
            pltpu.VMEM((3, NZ * RANK, BLOCK), BF16),
            pltpu.VMEM((CHUNKS, NC, NZ * PART, WIDE), F32),
            pltpu.VMEM((CHUNKS, NZ * PART, WIDE), F32),
            pltpu.VMEM((CHUNKS, NX, NZ * PART, LANES), F32),
            pltpu.VMEM((CHUNKS, NX - 1, NZ * PART, LANES), F32),
            pltpu.VMEM((CHUNKS, NZ * PART, LANES), F32),
            pltpu.VMEM((NY - 1, NZ * PART, LANES), F32),
            pltpu.VMEM((NZ, PART, LANES), F32),
            pltpu.VMEM((2, NZ - 1, PART, LANES), F32),
            pltpu.VMEM((NZ, BLOCK, HEAD), BF16),
            pltpu.VMEM((2, NC, NX, NY, PART, LANES), F32),
            pltpu.VMEM((2, CHUNKS, RANK, WIDE), F32),
            pltpu.VMEM((CHUNKS, RANK, WIDE), F32),
            pltpu.VMEM((RANK, RANK), F32),
            pltpu.VMEM((RANK, BLOCK), F32),
            pltpu.VMEM((RANK, BLOCK), F32),
            pltpu.VMEM((RANK, HEAD), F32),
            pltpu.VMEM((2, RANK, HEAD), F32),
            pltpu.VMEM((NX, PART, HEAD), F32),
            pltpu.VMEM((NY, PART, HEAD), F32),
            pltpu.VMEM((NY, PART, HEAD), F32),
            pltpu.VMEM((NX, PART, HEAD), F32),
            dma((CHUNKS,)), dma, dma, dma,
            dma((2, FAR)), dma((2, FAR, CHUNKS)),
            dma, dma,
            dma, dma((CHUNKS,)),
            dma, dma((CHUNKS,)),
            dma, dma,
            dma, dma((2,)),
            dma((3, 2)), dma((3, 2)),
            dma, dma,
            dma((5,)), dma((5,)),
        ],
        compiler_params=pltpu.CompilerParams(
            collective_id=0, has_side_effects=True, vmem_limit_bytes=40 * 2**20
        ),
    )(*[stay(array, pltpu.HBM) for array in (acts, grad_out, error[0], q_init.T)])
    new_error, q_t, p_t = pl.pallas_call(
        update_kernel,
        out_shape=(
            jax.ShapeDtypeStruct((D, HEAD), BF16),
            jax.ShapeDtypeStruct((RANK, HEAD), F32),
            jax.ShapeDtypeStruct((RANK, D), F32),
        ),
        in_specs=[vmem] * 4,
        out_specs=(hbm,) * 3,
        scratch_shapes=[pltpu.VMEM((D, HEAD), BF16), dma((CHUNKS + 2,))],
        compiler_params=pltpu.CompilerParams(vmem_limit_bytes=40 * 2**20),
    )(*[stay(array, pltpu.VMEM) for array in (merged, rows, q_t, p_t)])
    return new_error[None], q_t.T, p_t.T[None]


def solution(mesh):
    return jax.shard_map(
        per_device,
        mesh=mesh,
        in_specs=(
            P(("dp", "tensor"), None),
            P("dp", "tensor"),
            P("dp", None, "tensor"),
            P("tensor", None),
        ),
        out_specs=(P("dp", None, "tensor"), P("tensor", None), P("tensor", None, None)),
        check_vma=False,
    )
```

```python
import jax
import jax.numpy as jnp
from jax import lax
from jax.experimental import pallas as pl
from jax.experimental.pallas import tpu as pltpu
from jax.sharding import PartitionSpec as P

NX, NY, NC, NZ = 4, 8, 2, 8
D, HEAD, RANK, TOK = 4096, 128, 32, 1024
BLOCK = TOK // NZ
CHUNKS = 8
AHEAD = 2
FAR = NZ // 2
FAR_FIRST = (4, 3, 5, 2, 6, 1, 7)
WIDE = D // CHUNKS
LANES = WIDE // NX
PART = RANK // NC
F32, BF16 = jnp.float32, jnp.bfloat16
HIGHEST = lax.Precision.HIGHEST
MESH = pl.DeviceIdType.MESH
NT = ((1,), (1,))
NN = ((1,), (0,))
TN = ((0,), (0,))


def exact(a, b, dims=NN):
    return lax.dot_general(a, b, (dims, ((), ())), precision=HIGHEST, preferred_element_type=F32)


def single(a, b, dims=NN):
    return lax.dot_general(a, b, (dims, ((), ())), preferred_element_type=F32)


def split(value, parts):
    out = []
    for _ in range(parts):
        out.append(value.astype(BF16))
        value = value - out[-1].astype(F32)
    return out


def inverse_factor(gram):
    n = RANK
    row = lax.broadcasted_iota(jnp.int32, (n, n), 0)
    col = lax.broadcasted_iota(jnp.int32, (n, n), 1)
    both = jnp.concatenate([gram, jnp.where(row == col, 1.0, 0.0).astype(F32)], axis=1)
    rows = lax.broadcasted_iota(jnp.int32, (n, 1), 0)
    for j in range(n):
        inv = 1.0 / jnp.sqrt(both[j : j + 1, j : j + 1])
        pivot = both[j : j + 1, :] * inv
        factor = both[:, j : j + 1] * inv
        both = jnp.where(rows > j, both - factor * pivot, jnp.where(rows == j, pivot, both))
    return both[:, n:]


def kernel(
    acts, grad_out, error, q_init,
    merged, pb_rows, q_out, p_out,
    abuf, gbuf, ebuf, qbuf,
    w_out, w_in, w_split, partial, core_in, core_sum, x_in, x_sum, y_in, y_sum, z_in,
    gperm, pg, pt, pb, small, u_out, u_in, q_acc, q_core, qx_a, qy_a, qy_b, qx_b,
    load_sem, g_sem, e_sem, i_sem, z_send, z_recv, w_send, w_recv,
    c_send, c_recv, x_send, x_recv, y_send, y_recv, s_send, s_recv, p_send, p_recv, u_send, u_recv, q_send, q_recv,
):
    dp = lax.axis_index("dp")
    z = lax.axis_index("tensor")
    core = lax.rem(dp, NC)
    y = lax.rem(dp // NC, NY)
    x = dp // (NC * NY)

    def at(x_, y_, core_):
        return ((x_ * NY + y_) * NC + core_, z)

    sibling = at(x, y, 1 - core)
    ys = [at(x, lax.rem(y + k, NY), core) for k in FAR_FIRST]
    xs = [at(lax.rem(x + k, NX), y, core) for k in (2, 1, 3)]
    zs = [(dp, lax.rem(z + k, NZ)) for k in range(1, NZ)]
    up, down = zs[0], zs[-1]

    def to(ref_from, ref_to, send_sem, recv_sem, device):
        return pltpu.make_async_remote_copy(
            src_ref=ref_from, dst_ref=ref_to, send_sem=send_sem, recv_sem=recv_sem,
            device_id=device, device_id_type=MESH,
        )

    def wait_bytes(ref, sem):
        pltpu.make_async_copy(ref, ref, sem).wait()

    barrier = pltpu.get_barrier_semaphore()
    partners = [zs[k - 1] for k in FAR_FIRST] + ys + xs + [sibling]
    for device in partners:
        pl.semaphore_signal(barrier, inc=1, device_id=device, device_id_type=MESH)

    def load(c):
        columns = pl.ds(pl.multiple_of(c * WIDE, WIDE), WIDE)
        return pltpu.make_async_copy(acts.at[:, columns], abuf.at[c, 0], load_sem.at[c])

    load_q = pltpu.make_async_copy(q_init, qbuf, i_sem)
    load_g = pltpu.make_async_copy(grad_out, gbuf, g_sem)
    load_e = pltpu.make_async_copy(error, ebuf, e_sem)
    load_q.start()
    load_g.start()

    @pl.loop(0, CHUNKS)
    def _(c):
        load(c).start()

    load_e.start()

    def slot_of(hop, way):
        d = hop if way == 0 else (NZ - hop) % NZ
        return NZ - 1 if d == FAR else d - (d > FAR)

    def z_copy(c, hop, way):
        source = abuf.at[c, slot_of(hop - 1, way)]
        target = abuf.at[c, slot_of(hop, way)]
        if hop == FAR:
            part = pl.ds(way * (BLOCK // 2), BLOCK // 2)
            source, target = source.at[part], target.at[part]
        return to(source, target, z_send.at[way, hop - 1], z_recv.at[way, hop - 1, c], up if way == 0 else down)

    def own_send(c):
        for way in range(2):
            z_copy(c, 1, way).start()

    load_q.wait()
    load_g.wait()
    q_parts = jnp.concatenate(split(qbuf[...], 3), axis=0)
    w_all = single(q_parts, gbuf[...], NT)
    w_all = w_all[:RANK] + w_all[RANK : 2 * RANK] + w_all[2 * RANK :]
    for s in range(NZ):
        for h in range(NC):
            w_out[s, h] = w_all[h * PART : (h + 1) * PART, s * BLOCK : (s + 1) * BLOCK]

    @pl.loop(0, CHUNKS)
    def _(c):
        load(c).wait()

    pl.semaphore_wait(barrier, len(partners))

    def w_copy(k):
        return to(w_out.at[lax.rem(z + k, NZ)], w_in.at[:, z], w_send, w_recv, zs[k - 1])

    for k in FAR_FIRST:
        w_copy(k).start()
    w_in[:, z] = w_out[z]
    for c in range(AHEAD):
        own_send(c)

    for d in range(NZ):
        rows = pl.ds(pl.multiple_of(lax.rem(z + NZ - d, NZ) * BLOCK, BLOCK), BLOCK)
        place = NZ - 1 if d == FAR else d - (d > FAR)
        gperm[place] = gbuf[rows, :]


    def on(c, act):
        pl.when(jnp.logical_and(c >= 0, c < CHUNKS))(lambda: act(c))

    def forward(hop):
        def act(c):
            for way in range(2):
                z_copy(c, hop, way).wait_recv()
                z_copy(c, hop + 1, way).start()
        return act

    def rows_of(c):
        return pl.ds(pl.multiple_of(c * WIDE, WIDE), WIDE)

    def multiply(c):
        for way in range(2):
            z_copy(c, FAR - 1, way).wait_recv()
        near = NZ - 1
        grad = single(abuf[c, :near].reshape(near * BLOCK, WIDE), gperm[:near].reshape(near * BLOCK, HEAD), TN)
        merged[rows_of(c), :] = grad + ebuf[rows_of(c), :].astype(F32)

    def far_send(c):
        for way in range(2):
            z_copy(c, FAR, way).start()

    def finish(c):
        for way in range(2):
            z_copy(c, FAR, way).wait_recv()
        merged[rows_of(c), :] += single(abuf[c, NZ - 1], gperm[NZ - 1], TN)

    def w_ready():
        wait_bytes(w_in.at[:, pl.ds(0, NZ - 1)], w_recv)
        load_e.wait()
        w = w_in[...].reshape(NZ * RANK, BLOCK)
        for part, value in enumerate(split(w, 3)):
            w_split[part] = value

    def core_copy(i):
        return to(partial.at[i, 1 - core], core_in.at[i], c_send, c_recv.at[i], sibling)

    def p_partial(i):
        c = lax.rem(y + 1 + i, CHUNKS)
        a = abuf[c, 0]
        total = single(w_split[0], a) + (single(w_split[1], a) + single(w_split[2], a))
        partial[i] = total.reshape(NC, NZ * PART, WIDE)
        e_all = single(jnp.concatenate(split(qbuf[...], 3), axis=0), ebuf[rows_of(c), :], NT)
        e_all = e_all[:RANK] + (e_all[RANK : 2 * RANK] + e_all[2 * RANK :])
        mine = pl.ds(pl.multiple_of(z * PART, PART), PART)
        for h in range(NC):
            partial[i, h, mine, :] = partial[i, h, mine, :] + e_all[h * PART : (h + 1) * PART]
        core_copy(i).start()

    def p_core(i):
        core_copy(i).wait_recv()
        total = partial[i, core] + core_in[i]
        for j in range(NX):
            core_sum[i, j] = total[:, j * LANES : (j + 1) * LANES]
        for k, device in zip((2, 1, 3), xs):
            to(core_sum.at[i, lax.rem(x + k, NX)], x_in.at[i, k - 1], x_send, x_recv.at[i], device).start()

    def y_copy(i):
        device = at(x, lax.rem(y + 1 + i, NY), core)
        return to(x_sum.at[i], y_in.at[i], y_send, y_recv, device)

    def p_x(i):
        wait_bytes(x_in.at[i], x_recv.at[i])
        total = core_sum[i, x]
        for k in range(NX - 1):
            total = total + x_in[i, k]
        x_sum[i] = total
        pl.when(i < CHUNKS - 1)(lambda: y_copy(i).start())

    def s_copy(k, w):
        return to(y_sum.at[lax.rem(z + k + FAR * w, NZ)], z_in.at[w, k - 1], s_send, s_recv.at[w], zs[k - 1])

    def p_y():
        wait_bytes(y_in, y_recv)
        total = x_sum[CHUNKS - 1]
        for k in range(NY - 1):
            total = total + y_in[k]
        y_sum[...] = total.reshape(NZ, PART, LANES)
        for k in FAR_FIRST:
            for w in range(2):
                s_copy(k, w).start()

    def p_z():
        for w in range(2):
            wait_bytes(z_in.at[w], s_recv.at[w])
            total = y_sum[lax.rem(z + FAR * w, NZ)]
            for k in range(NZ - 1):
                total = total + z_in[w, k]
            mine = pg.at[w, core, x, y]
            mine[...] = total
            for device in ys:
                to(mine, mine, p_send.at[0, w], p_recv.at[0, w], device).start()

    def gather_x():
        for w in range(2):
            wait_bytes(pg.at[w, core, x, pl.ds(0, NY - 1)], p_recv.at[0, w])
            mine = pg.at[w, core, x]
            for device in xs:
                to(mine, mine, p_send.at[1, w], p_recv.at[1, w], device).start()

    def gather_core():
        for w in range(2):
            wait_bytes(pg.at[w, core, pl.ds(0, NX - 1)], p_recv.at[1, w])
            to(pg.at[w, core], pg.at[w, core], p_send.at[2, w], p_recv.at[2, w], sibling).start()

    def gather_done():
        for w in range(2):
            wait_bytes(pg.at[w, core], p_recv.at[2, w])

        @pl.loop(0, CHUNKS)
        def _(c):
            for w in range(2):
                for h in range(NC):
                    for j in range(NX):
                        pt[w, c, h * PART : (h + 1) * PART, j * LANES : (j + 1) * LANES] = pg[w, h, j, c]

    def u_copy():
        return to(u_out, u_in, u_send, u_recv, zs[FAR - 1])

    def three(stacked):
        return stacked[:RANK] + (stacked[RANK : 2 * RANK] + stacked[2 * RANK :])

    def u_make():
        u_out[...] = jnp.zeros_like(u_out)
        q_acc[...] = jnp.zeros_like(q_acc)

        @pl.loop(0, CHUNKS)
        def _(c):
            u_out[...] += three(single(jnp.concatenate(split(pt[1, c], 3), axis=0), abuf[c, 0], NT))

        u_copy().start()

    def u_use():
        u_copy().wait_recv()
        q_acc[...] += three(single(jnp.concatenate(split(u_in[...], 3), axis=0), gperm[NZ - 1]))

    def make_gram():
        tall = pt[0].reshape(CHUNKS * RANK, WIDE)
        square = exact(tall, tall, NT)
        gram = square[:RANK, :RANK]
        for c in range(1, CHUNKS):
            gram = gram + square[c * RANK : (c + 1) * RANK, c * RANK : (c + 1) * RANK]
        small[...] = gram

    def make_inverse():
        small[...] = inverse_factor(small[...])

    def basis():
        inverse = small[...]
        wide = jnp.concatenate([jnp.concatenate([inverse] * CHUNKS, axis=0)] * CHUNKS, axis=1)
        group_r = lax.broadcasted_iota(jnp.int32, wide.shape, 0) // RANK
        group_c = lax.broadcasted_iota(jnp.int32, wide.shape, 1) // RANK
        blocks = jnp.where(group_r == group_c, wide, 0.0)
        pb[...] = exact(blocks, pt[0].reshape(CHUNKS * RANK, WIDE)).reshape(CHUNKS, RANK, WIDE)

    def basis_rows():
        @pl.loop(0, CHUNKS)
        def _(c):
            value = pb[c]
            p_out[:, rows_of(c)] = value
            high, low = [part.astype(F32) for part in split(value, 2)]
            stacked = jnp.concatenate([high, low, high, low], axis=0)
            pb_rows[rows_of(c), :] = stacked.T.astype(BF16)

    def q_part(c):
        a = split(pt[0, c], 3)
        b = split(merged[rows_of(c), :], 3)
        first = three(single(jnp.concatenate(a, axis=0), b[0]))
        second = single(jnp.concatenate(a[:2], axis=0), b[1])
        q_acc[...] += first + (second[:RANK] + (second[RANK:] + single(a[0], b[2])))

    def q_early(start, end):
        @pl.loop(start, end)
        def _(c):
            q_part(c)

    def when(k, tick, *acts_):
        @pl.when(k == tick)
        def _():
            for act in acts_:
                act()

    @pl.loop(0, CHUNKS + 3)
    def _(k):
        on(k + AHEAD, own_send)
        step = 3 * k - 3
        when(k, 1, w_ready)
        on(step, p_partial)
        on(step - 2, p_x)
        on(k - 1, forward(1))
        on(step, p_core)
        on(step + 1, p_partial)
        on(step - 1, p_x)
        when(k, 8, gather_core)
        on(k - 2, forward(2))
        when(k, 9, *[lambda c=c: far_send(c) for c in range(6)])
        on(step + 1, p_core)
        on(step + 2, p_partial)
        when(k, 4, p_y)
        when(k, 5, p_z)
        when(k, 6, gather_x)
        when(k, 8, gather_done, u_make, lambda: q_early(0, 5))
        on(k - 3, multiply)
        on(step + 2, p_core)
        on(step, p_x)
        pl.when(k >= 8)(lambda: q_part(k - 3))

    u_use()
    q_core[0] = q_acc[...]
    q_c = to(q_core.at[0], q_core.at[1], q_send.at[0], q_recv.at[0], sibling)
    q_c.start()
    far_send(6)
    far_send(7)

    def share(buf, place, value, sem, devices):
        buf[place] = value
        for device in devices:
            to(buf.at[place], buf.at[place], q_send.at[sem], q_recv.at[sem], device).start()

    def total_of(buf, sem):
        n = buf.shape[0]
        wait_bytes(buf.at[pl.ds(0, n - 1)], q_recv.at[sem])
        total = buf[0]
        for k in range(1, n):
            total = total + buf[k]
        return total

    make_gram()
    q_c.wait_recv()
    both = q_core[0] + q_core[1]
    share(qy_b, y, both[PART:], 2, ys)
    share(qx_a, x, both[:PART], 1, xs)
    make_inverse()
    share(qy_a, y, total_of(qx_a, 1), 3, ys)
    basis()
    finish(0)
    share(qx_b, x, total_of(qy_b, 2), 4, xs)
    basis_rows()
    for c in range(1, CHUNKS - 1):
        finish(c)
    q_out[...] = exact(small[...], jnp.concatenate([total_of(qy_a, 3), total_of(qx_b, 4)], axis=0))
    finish(CHUNKS - 1)

    for way in range(2):
        for hop in range(1, FAR):
            wait_bytes(abuf.at[:, 0], z_send.at[way, hop - 1])
        wait_bytes(abuf.at[:, 0, pl.ds(0, BLOCK // 2)], z_send.at[way, FAR - 1])
    wait_bytes(w_in.at[:, pl.ds(0, NZ - 1)], w_send)
    wait_bytes(core_in, c_send)
    wait_bytes(x_in, x_send)
    wait_bytes(y_in, y_send)
    wait_bytes(z_in, s_send)
    for w in range(2):
        wait_bytes(pg.at[w, core, x, pl.ds(0, NY - 1)], p_send.at[0, w])
        wait_bytes(pg.at[w, core, pl.ds(0, NX - 1)], p_send.at[1, w])
        wait_bytes(pg.at[w, core], p_send.at[2, w])
    u_copy().wait_send()
    q_c.wait_send()
    wait_bytes(qx_a.at[pl.ds(0, NX - 1)], q_send.at[1])
    wait_bytes(qy_b.at[pl.ds(0, NY - 1)], q_send.at[2])
    wait_bytes(qy_a.at[pl.ds(0, NY - 1)], q_send.at[3])
    wait_bytes(qx_b.at[pl.ds(0, NX - 1)], q_send.at[4])


def update_kernel(merged, rows, q_t, p_t, new_error, q_out, p_out, buf, sems):
    save_q = pltpu.make_async_copy(q_t, q_out, sems.at[CHUNKS])
    save_p = pltpu.make_async_copy(p_t, p_out, sems.at[CHUNKS + 1])
    save_q.start()
    save_p.start()
    high, low = split(q_t[...] * (1.0 / (NX * NY * NC)), 2)
    back = jnp.concatenate([high, high, low, low], axis=0)

    def save(c):
        part = pl.ds(c * WIDE, WIDE)
        return pltpu.make_async_copy(buf.at[part], new_error.at[part], sems.at[c])

    for c in range(CHUNKS):
        part = pl.ds(c * WIDE, WIDE)
        buf[part, :] = (merged[part, :] - single(rows[part, :], back)).astype(BF16)
        save(c).start()
    for c in range(CHUNKS):
        save(c).wait()
    save_q.wait()
    save_p.wait()


def per_device(acts, grad_out, error, q_init):
    dma = pltpu.SemaphoreType.DMA
    hbm = pl.BlockSpec(memory_space=pltpu.HBM)
    vmem = pl.BlockSpec(memory_space=pltpu.VMEM)

    def stay(array, place):
        return pltpu.with_memory_space_constraint(array, place)

    merged, rows, q_t, p_t = pl.pallas_call(
        kernel,
        out_shape=(
            pltpu.VMEM((D, HEAD), F32),
            pltpu.VMEM((D, 4 * RANK), BF16),
            pltpu.VMEM((RANK, HEAD), F32),
            pltpu.VMEM((RANK, D), F32),
        ),
        in_specs=[hbm] * 4,
        out_specs=(vmem,) * 4,
        scratch_shapes=[
            pltpu.VMEM((CHUNKS, NZ, BLOCK, WIDE), BF16),
            pltpu.VMEM((TOK, HEAD), BF16),
            pltpu.VMEM((D, HEAD), BF16),
            pltpu.VMEM((RANK, HEAD), F32),
            pltpu.VMEM((NZ, NC, PART, BLOCK), F32),
            pltpu.VMEM((NC, NZ, PART, BLOCK), F32),
            pltpu.VMEM((3, NZ * RANK, BLOCK), BF16),
            pltpu.VMEM((CHUNKS, NC, NZ * PART, WIDE), F32),
            pltpu.VMEM((CHUNKS, NZ * PART, WIDE), F32),
            pltpu.VMEM((CHUNKS, NX, NZ * PART, LANES), F32),
            pltpu.VMEM((CHUNKS, NX - 1, NZ * PART, LANES), F32),
            pltpu.VMEM((CHUNKS, NZ * PART, LANES), F32),
            pltpu.VMEM((NY - 1, NZ * PART, LANES), F32),
            pltpu.VMEM((NZ, PART, LANES), F32),
            pltpu.VMEM((2, NZ - 1, PART, LANES), F32),
            pltpu.VMEM((NZ, BLOCK, HEAD), BF16),
            pltpu.VMEM((2, NC, NX, NY, PART, LANES), F32),
            pltpu.VMEM((2, CHUNKS, RANK, WIDE), F32),
            pltpu.VMEM((CHUNKS, RANK, WIDE), F32),
            pltpu.VMEM((RANK, RANK), F32),
            pltpu.VMEM((RANK, BLOCK), F32),
            pltpu.VMEM((RANK, BLOCK), F32),
            pltpu.VMEM((RANK, HEAD), F32),
            pltpu.VMEM((2, RANK, HEAD), F32),
            pltpu.VMEM((NX, PART, HEAD), F32),
            pltpu.VMEM((NY, PART, HEAD), F32),
            pltpu.VMEM((NY, PART, HEAD), F32),
            pltpu.VMEM((NX, PART, HEAD), F32),
            dma((CHUNKS,)), dma, dma, dma,
            dma((2, FAR)), dma((2, FAR, CHUNKS)),
            dma, dma,
            dma, dma((CHUNKS,)),
            dma, dma((CHUNKS,)),
            dma, dma,
            dma, dma((2,)),
            dma((3, 2)), dma((3, 2)),
            dma, dma,
            dma((5,)), dma((5,)),
        ],
        compiler_params=pltpu.CompilerParams(
            collective_id=0, has_side_effects=True, vmem_limit_bytes=40 * 2**20
        ),
    )(*[stay(array, pltpu.HBM) for array in (acts, grad_out, error[0], q_init.T)])
    new_error, q_t, p_t = pl.pallas_call(
        update_kernel,
        out_shape=(
            jax.ShapeDtypeStruct((D, HEAD), BF16),
            jax.ShapeDtypeStruct((RANK, HEAD), F32),
            jax.ShapeDtypeStruct((RANK, D), F32),
        ),
        in_specs=[vmem] * 4,
        out_specs=(hbm,) * 3,
        scratch_shapes=[pltpu.VMEM((D, HEAD), BF16), dma((CHUNKS + 2,))],
        compiler_params=pltpu.CompilerParams(vmem_limit_bytes=40 * 2**20),
    )(*[stay(array, pltpu.VMEM) for array in (merged, rows, q_t, p_t)])
    return new_error[None], q_t.T, p_t.T[None]


def solution(mesh):
    return jax.shard_map(
        per_device,
        mesh=mesh,
        in_specs=(
            P(("dp", "tensor"), None),
            P("dp", "tensor"),
            P("dp", None, "tensor"),
            P("tensor", None),
        ),
        out_specs=(P("dp", None, "tensor"), P("tensor", None), P("tensor", None, None)),
        check_vma=False,
    )
```

```python
import jax
import jax.numpy as jnp
from jax import lax
from jax.experimental import pallas as pl
from jax.experimental.pallas import tpu as pltpu
from jax.sharding import PartitionSpec as P

NX, NY, NC, NZ = 4, 8, 2, 8
D, HEAD, RANK, TOK = 4096, 128, 32, 1024
BLOCK = TOK // NZ
CHUNKS = 8
AHEAD = 2
FAR = NZ // 2
FAR_FIRST = (4, 3, 5, 2, 6, 1, 7)
WIDE = D // CHUNKS
LANES = WIDE // NX
PART = RANK // NC
F32, BF16 = jnp.float32, jnp.bfloat16
HIGHEST = lax.Precision.HIGHEST
MESH = pl.DeviceIdType.MESH
NT = ((1,), (1,))
NN = ((1,), (0,))
TN = ((0,), (0,))


def exact(a, b, dims=NN):
    return lax.dot_general(a, b, (dims, ((), ())), precision=HIGHEST, preferred_element_type=F32)


def single(a, b, dims=NN):
    return lax.dot_general(a, b, (dims, ((), ())), preferred_element_type=F32)


def split(value, parts):
    out = []
    for _ in range(parts):
        out.append(value.astype(BF16))
        value = value - out[-1].astype(F32)
    return out


def inverse_factor(gram):
    n = RANK
    row = lax.broadcasted_iota(jnp.int32, (n, n), 0)
    col = lax.broadcasted_iota(jnp.int32, (n, n), 1)
    both = jnp.concatenate([gram, jnp.where(row == col, 1.0, 0.0).astype(F32)], axis=1)
    rows = lax.broadcasted_iota(jnp.int32, (n, 1), 0)
    for j in range(n):
        inv = 1.0 / jnp.sqrt(both[j : j + 1, j : j + 1])
        pivot = both[j : j + 1, :] * inv
        factor = both[:, j : j + 1] * inv
        both = jnp.where(rows > j, both - factor * pivot, jnp.where(rows == j, pivot, both))
    return both[:, n:]


def kernel(
    acts, grad_out, error, q_init,
    merged, pb_rows, q_out, p_out,
    abuf, gbuf, ebuf, qbuf,
    w_out, w_in, w_split, partial, core_in, core_sum, x_in, x_sum, y_in, y_sum, z_in,
    gperm, pg, pt, pb, small, u_out, u_in, q_acc, q_core, qx_a, qy_a, qy_b, qx_b,
    load_sem, g_sem, e_sem, i_sem, z_send, z_recv, w_send, w_recv,
    c_send, c_recv, x_send, x_recv, y_send, y_recv, s_send, s_recv, p_send, p_recv, u_send, u_recv, q_send, q_recv,
):
    dp = lax.axis_index("dp")
    z = lax.axis_index("tensor")
    core = lax.rem(dp, NC)
    y = lax.rem(dp // NC, NY)
    x = dp // (NC * NY)

    def at(x_, y_, core_):
        return ((x_ * NY + y_) * NC + core_, z)

    sibling = at(x, y, 1 - core)
    ys = [at(x, lax.rem(y + k, NY), core) for k in FAR_FIRST]
    xs = [at(lax.rem(x + k, NX), y, core) for k in (2, 1, 3)]
    zs = [(dp, lax.rem(z + k, NZ)) for k in range(1, NZ)]
    up, down = zs[0], zs[-1]

    def to(ref_from, ref_to, send_sem, recv_sem, device):
        return pltpu.make_async_remote_copy(
            src_ref=ref_from, dst_ref=ref_to, send_sem=send_sem, recv_sem=recv_sem,
            device_id=device, device_id_type=MESH,
        )

    def wait_bytes(ref, sem):
        pltpu.make_async_copy(ref, ref, sem).wait()

    barrier = pltpu.get_barrier_semaphore()
    partners = [zs[k - 1] for k in FAR_FIRST] + ys + xs + [sibling]
    for device in partners:
        pl.semaphore_signal(barrier, inc=1, device_id=device, device_id_type=MESH)

    def load(c):
        columns = pl.ds(pl.multiple_of(c * WIDE, WIDE), WIDE)
        return pltpu.make_async_copy(acts.at[:, columns], abuf.at[c, 0], load_sem.at[c])

    load_q = pltpu.make_async_copy(q_init, qbuf, i_sem)
    load_g = pltpu.make_async_copy(grad_out, gbuf, g_sem)
    load_e = pltpu.make_async_copy(error, ebuf, e_sem)
    load_q.start()
    load_g.start()

    @pl.loop(0, CHUNKS)
    def _(c):
        load(c).start()

    load_e.start()

    def slot_of(hop, way):
        d = hop if way == 0 else (NZ - hop) % NZ
        return NZ - 1 if d == FAR else d - (d > FAR)

    def z_copy(c, hop, way):
        source = abuf.at[c, slot_of(hop - 1, way)]
        target = abuf.at[c, slot_of(hop, way)]
        if hop == FAR:
            part = pl.ds(way * (BLOCK // 2), BLOCK // 2)
            source, target = source.at[part], target.at[part]
        return to(source, target, z_send.at[way, hop - 1], z_recv.at[way, hop - 1, c], up if way == 0 else down)

    def own_send(c):
        for way in range(2):
            z_copy(c, 1, way).start()

    load_q.wait()
    load_g.wait()
    q_parts = jnp.concatenate(split(qbuf[...], 3), axis=0)
    w_all = single(q_parts, gbuf[...], NT)
    w_all = w_all[:RANK] + w_all[RANK : 2 * RANK] + w_all[2 * RANK :]
    for s in range(NZ):
        for h in range(NC):
            w_out[s, h] = w_all[h * PART : (h + 1) * PART, s * BLOCK : (s + 1) * BLOCK]

    @pl.loop(0, CHUNKS)
    def _(c):
        load(c).wait()

    pl.semaphore_wait(barrier, len(partners))

    def w_copy(k):
        return to(w_out.at[lax.rem(z + k, NZ)], w_in.at[:, z], w_send, w_recv, zs[k - 1])

    for k in FAR_FIRST:
        w_copy(k).start()
    w_in[:, z] = w_out[z]
    for c in range(AHEAD):
        own_send(c)

    for d in range(NZ):
        rows = pl.ds(pl.multiple_of(lax.rem(z + NZ - d, NZ) * BLOCK, BLOCK), BLOCK)
        place = NZ - 1 if d == FAR else d - (d > FAR)
        gperm[place] = gbuf[rows, :]


    def on(c, act):
        pl.when(jnp.logical_and(c >= 0, c < CHUNKS))(lambda: act(c))

    def forward(hop):
        def act(c):
            for way in range(2):
                z_copy(c, hop, way).wait_recv()
                z_copy(c, hop + 1, way).start()
        return act

    def rows_of(c):
        return pl.ds(pl.multiple_of(c * WIDE, WIDE), WIDE)

    def multiply(c):
        for way in range(2):
            z_copy(c, FAR - 1, way).wait_recv()
        near = NZ - 1
        grad = single(abuf[c, :near].reshape(near * BLOCK, WIDE), gperm[:near].reshape(near * BLOCK, HEAD), TN)
        merged[rows_of(c), :] = grad + ebuf[rows_of(c), :].astype(F32)

    def far_send(c):
        for way in range(2):
            z_copy(c, FAR, way).start()

    def finish(c):
        for way in range(2):
            z_copy(c, FAR, way).wait_recv()
        merged[rows_of(c), :] += single(abuf[c, NZ - 1], gperm[NZ - 1], TN)

    def w_ready():
        wait_bytes(w_in.at[:, pl.ds(0, NZ - 1)], w_recv)
        load_e.wait()
        w = w_in[...].reshape(NZ * RANK, BLOCK)
        for part, value in enumerate(split(w, 3)):
            w_split[part] = value

    def core_copy(i):
        return to(partial.at[i, 1 - core], core_in.at[i], c_send, c_recv.at[i], sibling)

    def p_partial(i):
        c = lax.rem(y + 1 + i, CHUNKS)
        a = abuf[c, 0]
        total = single(w_split[0], a) + (single(w_split[1], a) + single(w_split[2], a))
        partial[i] = total.reshape(NC, NZ * PART, WIDE)
        e_all = single(jnp.concatenate(split(qbuf[...], 3), axis=0), ebuf[rows_of(c), :], NT)
        e_all = e_all[:RANK] + (e_all[RANK : 2 * RANK] + e_all[2 * RANK :])
        mine = pl.ds(pl.multiple_of(z * PART, PART), PART)
        for h in range(NC):
            partial[i, h, mine, :] = partial[i, h, mine, :] + e_all[h * PART : (h + 1) * PART]
        core_copy(i).start()

    def p_core(i):
        core_copy(i).wait_recv()
        total = partial[i, core] + core_in[i]
        for j in range(NX):
            core_sum[i, j] = total[:, j * LANES : (j + 1) * LANES]
        for k, device in zip((2, 1, 3), xs):
            to(core_sum.at[i, lax.rem(x + k, NX)], x_in.at[i, k - 1], x_send, x_recv.at[i], device).start()

    def y_copy(i):
        device = at(x, lax.rem(y + 1 + i, NY), core)
        return to(x_sum.at[i], y_in.at[i], y_send, y_recv, device)

    def p_x(i):
        wait_bytes(x_in.at[i], x_recv.at[i])
        total = core_sum[i, x]
        for k in range(NX - 1):
            total = total + x_in[i, k]
        x_sum[i] = total
        pl.when(i < CHUNKS - 1)(lambda: y_copy(i).start())

    def s_copy(k, w):
        return to(y_sum.at[lax.rem(z + k + FAR * w, NZ)], z_in.at[w, k - 1], s_send, s_recv.at[w], zs[k - 1])

    def p_y():
        wait_bytes(y_in, y_recv)
        total = x_sum[CHUNKS - 1]
        for k in range(NY - 1):
            total = total + y_in[k]
        y_sum[...] = total.reshape(NZ, PART, LANES)
        for k in FAR_FIRST:
            for w in range(2):
                s_copy(k, 1 - w).start()

    def p_z():
        for w in (1, 0):
            wait_bytes(z_in.at[w], s_recv.at[w])
            total = y_sum[lax.rem(z + FAR * w, NZ)]
            for k in range(NZ - 1):
                total = total + z_in[w, k]
            mine = pg.at[w, core, x, y]
            mine[...] = total
            for device in ys:
                to(mine, mine, p_send.at[0, w], p_recv.at[0, w], device).start()

    def gather_x():
        for w in (1, 0):
            wait_bytes(pg.at[w, core, x, pl.ds(0, NY - 1)], p_recv.at[0, w])
            mine = pg.at[w, core, x]
            for device in xs:
                to(mine, mine, p_send.at[1, w], p_recv.at[1, w], device).start()

    def gather_core():
        for w in (1, 0):
            wait_bytes(pg.at[w, core, pl.ds(0, NX - 1)], p_recv.at[1, w])
            to(pg.at[w, core], pg.at[w, core], p_send.at[2, w], p_recv.at[2, w], sibling).start()

    def gather_done(w):
        wait_bytes(pg.at[w, core], p_recv.at[2, w])

        @pl.loop(0, CHUNKS)
        def _(c):
            for h in range(NC):
                for j in range(NX):
                    pt[w, c, h * PART : (h + 1) * PART, j * LANES : (j + 1) * LANES] = pg[w, h, j, c]

    def u_copy():
        return to(u_out, u_in, u_send, u_recv, zs[FAR - 1])

    def three(stacked):
        return stacked[:RANK] + (stacked[RANK : 2 * RANK] + stacked[2 * RANK :])

    def u_make():
        u_out[...] = jnp.zeros_like(u_out)
        q_acc[...] = jnp.zeros_like(q_acc)

        @pl.loop(0, CHUNKS)
        def _(c):
            u_out[...] += three(single(jnp.concatenate(split(pt[1, c], 3), axis=0), abuf[c, 0], NT))

        u_copy().start()

    def u_use():
        u_copy().wait_recv()
        q_acc[...] += three(single(jnp.concatenate(split(u_in[...], 3), axis=0), gperm[NZ - 1]))

    def make_gram():
        tall = pt[0].reshape(CHUNKS * RANK, WIDE)
        square = exact(tall, tall, NT)
        gram = square[:RANK, :RANK]
        for c in range(1, CHUNKS):
            gram = gram + square[c * RANK : (c + 1) * RANK, c * RANK : (c + 1) * RANK]
        small[...] = gram

    def make_inverse():
        small[...] = inverse_factor(small[...])

    def basis():
        inverse = small[...]
        wide = jnp.concatenate([jnp.concatenate([inverse] * CHUNKS, axis=0)] * CHUNKS, axis=1)
        group_r = lax.broadcasted_iota(jnp.int32, wide.shape, 0) // RANK
        group_c = lax.broadcasted_iota(jnp.int32, wide.shape, 1) // RANK
        blocks = jnp.where(group_r == group_c, wide, 0.0)
        pb[...] = exact(blocks, pt[0].reshape(CHUNKS * RANK, WIDE)).reshape(CHUNKS, RANK, WIDE)

    def basis_rows():
        @pl.loop(0, CHUNKS)
        def _(c):
            value = pb[c]
            p_out[:, rows_of(c)] = value
            high, low = [part.astype(F32) for part in split(value, 2)]
            stacked = jnp.concatenate([high, low, high, low], axis=0)
            pb_rows[rows_of(c), :] = stacked.T.astype(BF16)

    def q_part(c):
        a = split(pt[0, c], 3)
        b = split(merged[rows_of(c), :], 3)
        first = three(single(jnp.concatenate(a, axis=0), b[0]))
        second = single(jnp.concatenate(a[:2], axis=0), b[1])
        q_acc[...] += first + (second[:RANK] + (second[RANK:] + single(a[0], b[2])))

    def q_early(start, end):
        @pl.loop(start, end)
        def _(c):
            q_part(c)

    def when(k, tick, *acts_):
        @pl.when(k == tick)
        def _():
            for act in acts_:
                act()

    @pl.loop(0, CHUNKS + 3)
    def _(k):
        on(k + AHEAD, own_send)
        step = 3 * k - 3
        when(k, 1, w_ready)
        on(step, p_partial)
        on(step - 2, p_x)
        on(k - 1, forward(1))
        on(step, p_core)
        on(step + 1, p_partial)
        on(step - 1, p_x)
        when(k, 8, gather_core)
        on(k - 2, forward(2))
        when(k, 9, *[lambda c=c: far_send(c) for c in range(6)])
        on(step + 1, p_core)
        on(step + 2, p_partial)
        when(k, 4, p_y)
        when(k, 5, p_z)
        when(k, 6, gather_x)
        when(k, 8, lambda: gather_done(1), u_make, lambda: gather_done(0), lambda: q_early(0, 5))
        on(k - 3, multiply)
        on(step + 2, p_core)
        on(step, p_x)
        pl.when(k >= 8)(lambda: q_part(k - 3))

    u_use()
    q_core[0] = q_acc[...]
    q_c = to(q_core.at[0], q_core.at[1], q_send.at[0], q_recv.at[0], sibling)
    q_c.start()
    far_send(6)
    far_send(7)

    def share(buf, place, value, sem, devices):
        buf[place] = value
        for device in devices:
            to(buf.at[place], buf.at[place], q_send.at[sem], q_recv.at[sem], device).start()

    def total_of(buf, sem):
        n = buf.shape[0]
        wait_bytes(buf.at[pl.ds(0, n - 1)], q_recv.at[sem])
        total = buf[0]
        for k in range(1, n):
            total = total + buf[k]
        return total

    make_gram()
    q_c.wait_recv()
    both = q_core[0] + q_core[1]
    share(qy_b, y, both[PART:], 2, ys)
    share(qx_a, x, both[:PART], 1, xs)
    make_inverse()
    share(qy_a, y, total_of(qx_a, 1), 3, ys)
    basis()
    finish(0)
    share(qx_b, x, total_of(qy_b, 2), 4, xs)
    basis_rows()
    for c in range(1, CHUNKS - 1):
        finish(c)
    q_out[...] = exact(small[...], jnp.concatenate([total_of(qy_a, 3), total_of(qx_b, 4)], axis=0))
    finish(CHUNKS - 1)

    for way in range(2):
        for hop in range(1, FAR):
            wait_bytes(abuf.at[:, 0], z_send.at[way, hop - 1])
        wait_bytes(abuf.at[:, 0, pl.ds(0, BLOCK // 2)], z_send.at[way, FAR - 1])
    wait_bytes(w_in.at[:, pl.ds(0, NZ - 1)], w_send)
    wait_bytes(core_in, c_send)
    wait_bytes(x_in, x_send)
    wait_bytes(y_in, y_send)
    wait_bytes(z_in, s_send)
    for w in range(2):
        wait_bytes(pg.at[w, core, x, pl.ds(0, NY - 1)], p_send.at[0, w])
        wait_bytes(pg.at[w, core, pl.ds(0, NX - 1)], p_send.at[1, w])
        wait_bytes(pg.at[w, core], p_send.at[2, w])
    u_copy().wait_send()
    q_c.wait_send()
    wait_bytes(qx_a.at[pl.ds(0, NX - 1)], q_send.at[1])
    wait_bytes(qy_b.at[pl.ds(0, NY - 1)], q_send.at[2])
    wait_bytes(qy_a.at[pl.ds(0, NY - 1)], q_send.at[3])
    wait_bytes(qx_b.at[pl.ds(0, NX - 1)], q_send.at[4])


def update_kernel(merged, rows, q_t, p_t, new_error, q_out, p_out, buf, sems):
    save_q = pltpu.make_async_copy(q_t, q_out, sems.at[CHUNKS])
    save_p = pltpu.make_async_copy(p_t, p_out, sems.at[CHUNKS + 1])
    save_q.start()
    save_p.start()
    high, low = split(q_t[...] * (1.0 / (NX * NY * NC)), 2)
    back = jnp.concatenate([high, high, low, low], axis=0)

    def save(c):
        part = pl.ds(c * WIDE, WIDE)
        return pltpu.make_async_copy(buf.at[part], new_error.at[part], sems.at[c])

    for c in range(CHUNKS):
        part = pl.ds(c * WIDE, WIDE)
        buf[part, :] = (merged[part, :] - single(rows[part, :], back)).astype(BF16)
        save(c).start()
    for c in range(CHUNKS):
        save(c).wait()
    save_q.wait()
    save_p.wait()


def per_device(acts, grad_out, error, q_init):
    dma = pltpu.SemaphoreType.DMA
    hbm = pl.BlockSpec(memory_space=pltpu.HBM)
    vmem = pl.BlockSpec(memory_space=pltpu.VMEM)

    def stay(array, place):
        return pltpu.with_memory_space_constraint(array, place)

    merged, rows, q_t, p_t = pl.pallas_call(
        kernel,
        out_shape=(
            pltpu.VMEM((D, HEAD), F32),
            pltpu.VMEM((D, 4 * RANK), BF16),
            pltpu.VMEM((RANK, HEAD), F32),
            pltpu.VMEM((RANK, D), F32),
        ),
        in_specs=[hbm] * 4,
        out_specs=(vmem,) * 4,
        scratch_shapes=[
            pltpu.VMEM((CHUNKS, NZ, BLOCK, WIDE), BF16),
            pltpu.VMEM((TOK, HEAD), BF16),
            pltpu.VMEM((D, HEAD), BF16),
            pltpu.VMEM((RANK, HEAD), F32),
            pltpu.VMEM((NZ, NC, PART, BLOCK), F32),
            pltpu.VMEM((NC, NZ, PART, BLOCK), F32),
            pltpu.VMEM((3, NZ * RANK, BLOCK), BF16),
            pltpu.VMEM((CHUNKS, NC, NZ * PART, WIDE), F32),
            pltpu.VMEM((CHUNKS, NZ * PART, WIDE), F32),
            pltpu.VMEM((CHUNKS, NX, NZ * PART, LANES), F32),
            pltpu.VMEM((CHUNKS, NX - 1, NZ * PART, LANES), F32),
            pltpu.VMEM((CHUNKS, NZ * PART, LANES), F32),
            pltpu.VMEM((NY - 1, NZ * PART, LANES), F32),
            pltpu.VMEM((NZ, PART, LANES), F32),
            pltpu.VMEM((2, NZ - 1, PART, LANES), F32),
            pltpu.VMEM((NZ, BLOCK, HEAD), BF16),
            pltpu.VMEM((2, NC, NX, NY, PART, LANES), F32),
            pltpu.VMEM((2, CHUNKS, RANK, WIDE), F32),
            pltpu.VMEM((CHUNKS, RANK, WIDE), F32),
            pltpu.VMEM((RANK, RANK), F32),
            pltpu.VMEM((RANK, BLOCK), F32),
            pltpu.VMEM((RANK, BLOCK), F32),
            pltpu.VMEM((RANK, HEAD), F32),
            pltpu.VMEM((2, RANK, HEAD), F32),
            pltpu.VMEM((NX, PART, HEAD), F32),
            pltpu.VMEM((NY, PART, HEAD), F32),
            pltpu.VMEM((NY, PART, HEAD), F32),
            pltpu.VMEM((NX, PART, HEAD), F32),
            dma((CHUNKS,)), dma, dma, dma,
            dma((2, FAR)), dma((2, FAR, CHUNKS)),
            dma, dma,
            dma, dma((CHUNKS,)),
            dma, dma((CHUNKS,)),
            dma, dma,
            dma, dma((2,)),
            dma((3, 2)), dma((3, 2)),
            dma, dma,
            dma((5,)), dma((5,)),
        ],
        compiler_params=pltpu.CompilerParams(
            collective_id=0, has_side_effects=True, vmem_limit_bytes=40 * 2**20
        ),
    )(*[stay(array, pltpu.HBM) for array in (acts, grad_out, error[0], q_init.T)])
    new_error, q_t, p_t = pl.pallas_call(
        update_kernel,
        out_shape=(
            jax.ShapeDtypeStruct((D, HEAD), BF16),
            jax.ShapeDtypeStruct((RANK, HEAD), F32),
            jax.ShapeDtypeStruct((RANK, D), F32),
        ),
        in_specs=[vmem] * 4,
        out_specs=(hbm,) * 3,
        scratch_shapes=[pltpu.VMEM((D, HEAD), BF16), dma((CHUNKS + 2,))],
        compiler_params=pltpu.CompilerParams(vmem_limit_bytes=40 * 2**20),
    )(*[stay(array, pltpu.VMEM) for array in (merged, rows, q_t, p_t)])
    return new_error[None], q_t.T, p_t.T[None]


def solution(mesh):
    return jax.shard_map(
        per_device,
        mesh=mesh,
        in_specs=(
            P(("dp", "tensor"), None),
            P("dp", "tensor"),
            P("dp", None, "tensor"),
            P("tensor", None),
        ),
        out_specs=(P("dp", None, "tensor"), P("tensor", None), P("tensor", None, None)),
        check_vma=False,
    )
```
